256 devices in a mesh: row: 16 (over x_lo, y, core), col: 16 (over x_hi, z).
Axes of the slice: x: 4 (x_hi: 2, x_lo: 2; x = x_hi * 2 + x_lo), y: 4, z: 8, core: 2. Of those that a mesh axis runs over, the one named last changes fastest.
Arguments:
- object_slices: float32 [2, 2, 2048, 2048], P(None, None, 'row', 'col'), may hold values from -4 to 4
- probe: float32 [2, 128, 128], replicated, may hold values from -5 to 5
- phase: float32 [128, 128], replicated, may hold values from -3.140625 to 3.140625
- positions: int32 [16, 16, 4, 2], P('row', 'col'), may hold values from 0 to 127
- counts: int32 [16, 16], P('row', 'col'), may hold values from 1 to 4
- measured: float32 [16, 16, 4, 128, 128], P('row', 'col'), may hold values from 0.2 to 4
Outputs:
- updated: float32 [2, 2, 2048, 2048], P(None, None, 'row', 'col')
The draws below stay inside these ranges and needn't reach their ends.
Inputs may be any that keep to these rules, and one draw needn't show every extreme that they name: Slots k with k >= counts of the tile are padding and do not contribute. `positions`: a window may reach up to 127 pixels into the tiles below, to the right and diagonally below right.
All inputs are finite; a program needn't handle non-finite values.
Results may differ from the reference program's by a relative error of at most 0.0003.
Values sent between devices are 32-bit elements; how exact they have to be, the bound alone decides.
A program may use at most 64 MiB of HBM per device.

```python
import math
import jax
import jax.numpy as jnp
from jax import lax

TILE = 128
WINDOW_PIXELS = 128
PROBE_SLOTS = 4
SLICES = 2
ITERS = 2
NR = 2048
NC = 2048
N_ROW = 16
N_COL = 16


def touch_ends(entries, stream_key, least, top_value):
    dims = entries.shape
    place = [jax.random.randint(jax.random.fold_in(stream_key, axis), (), 0, dims[axis]) for axis in range(len(dims))]
    entries = entries.at[tuple(place)].set(least)
    longest = dims.index(max(dims))
    place[longest] = (place[longest] + 1) % dims[longest]
    return entries.at[tuple(place)].set(top_value)


def block_scale(rng, dims, pieces, low, high):
    gain, own = 1.0, jax.random.fold_in(rng, 6)
    for axis_at, shards_of in pieces:
        draws = jnp.exp(jax.random.uniform(jax.random.fold_in(own, axis_at), (shards_of,), jnp.float32, low / len(pieces), high / len(pieces)))
        gain = gain * jnp.repeat(draws, dims[axis_at] // shards_of).reshape([-1 if axis == axis_at else 1 for axis in range(len(dims))])
    return gain


def bell_draw(key, dims, scale, most, cuts=(), kind=jnp.bfloat16):
    gain = block_scale(key, dims, cuts, -0.22, 0.18) if cuts else 1.0
    drawn = jax.random.normal(key, dims, jnp.float32) * scale * gain
    return jnp.minimum(jnp.maximum(drawn, -most), most).astype(kind)


def setup_inputs(seed: int = 0) -> dict:
    keys = jax.random.split(jax.random.key(seed), 7)
    object_slices = bell_draw(keys[0], (SLICES, 2, NR, NC), 0.7, 4.0, ((2, 16), (3, 16)), jnp.float32)
    probe = bell_draw(keys[1], (2, WINDOW_PIXELS, WINDOW_PIXELS), 1.0, 5.0, (), jnp.float32)
    phase = jnp.clip(jax.random.uniform(keys[2], (WINDOW_PIXELS, WINDOW_PIXELS), jnp.float32, -3.140625, 3.140625), -3.140625, 3.140625)
    positions = touch_ends(jax.random.randint(keys[3], (N_ROW, N_COL, PROBE_SLOTS, 2), 0, TILE), jax.random.fold_in(keys[3], 1), 0, TILE - 1).astype(jnp.int32)
    counts = touch_ends(jax.random.randint(keys[4], (N_ROW, N_COL), 1, PROBE_SLOTS + 1), jax.random.fold_in(keys[4], 1), 1, PROBE_SLOTS).astype(jnp.int32)
    measured = jnp.clip(jnp.exp(math.log(4.0) - 2.9957323 * jax.random.uniform(keys[5], (N_ROW, N_COL, PROBE_SLOTS, WINDOW_PIXELS, WINDOW_PIXELS), jnp.float32) ** block_scale(keys[5], (N_ROW, N_COL, PROBE_SLOTS, WINDOW_PIXELS, WINDOW_PIXELS), ((0, 16), (1, 16)), -0.2, 0.2)), 0.2, 4.0)
    return dict(object_slices=object_slices, probe=probe, phase=phase, positions=positions, counts=counts, measured=measured)


step_rate = 0.02

def dft_tables(width):
    index = jnp.arange(width, dtype=jnp.int32)
    product = index[:, None] * index[None, :] % width
    angle = product.astype(jnp.float32) * (-2.0 * jnp.pi / width)
    scale = 1.0 / jnp.sqrt(jnp.float32(width))
    return (jnp.cos(angle) * scale, jnp.sin(angle) * scale)

def transform(real, imag, table_re, table_im):
    high = lax.Precision.HIGHEST
    left_re = jnp.einsum('ij,njk->nik', table_re, real, precision=high) - jnp.einsum('ij,njk->nik', table_im, imag, precision=high)
    left_im = jnp.einsum('ij,njk->nik', table_re, imag, precision=high) + jnp.einsum('ij,njk->nik', table_im, real, precision=high)
    out_re = jnp.einsum('nij,jk->nik', left_re, table_re, precision=high) - jnp.einsum('nij,jk->nik', left_im, table_im, precision=high)
    out_im = jnp.einsum('nij,jk->nik', left_re, table_im, precision=high) + jnp.einsum('nij,jk->nik', left_im, table_re, precision=high)
    return (out_re, out_im)

def local_loss(extended, positions, live, probe, phase, measured):
    width = probe.shape[-1]
    layers = extended.shape[0]
    table_re, table_im = dft_tables(width)

    def window(corner):
        corner = corner.astype(jnp.int32)
        zero = jnp.zeros((), jnp.int32)
        return lax.dynamic_slice(extended, (zero, zero, corner[0], corner[1]), (layers, 2, width, width))
    windows = jax.vmap(window)(positions)
    wave_re = jnp.broadcast_to(probe[0], windows[:, 0, 0].shape)
    wave_im = jnp.broadcast_to(probe[1], windows[:, 0, 0].shape)
    prop_re = jnp.cos(phase)
    prop_im = jnp.sin(phase)
    for layer in range(layers):
        obj_re = windows[:, layer, 0]
        obj_im = windows[:, layer, 1]
        wave_re, wave_im = (wave_re * obj_re - wave_im * obj_im, wave_re * obj_im + wave_im * obj_re)
        if layer + 1 < layers:
            spec_re, spec_im = transform(wave_re, wave_im, table_re, table_im)
            spec_re, spec_im = (spec_re * prop_re - spec_im * prop_im, spec_re * prop_im + spec_im * prop_re)
            wave_re, wave_im = transform(spec_re, spec_im, table_re, -table_im)
    far_re, far_im = transform(wave_re, wave_im, table_re, table_im)
    misfit = far_re * far_re + far_im * far_im - measured
    return 0.5 * jnp.sum(live[:, None, None] * misfit * misfit)

def tile_gradient(extended, positions, count, measured, probe, phase):
    slots = positions.shape[0]
    live = (jnp.arange(slots, dtype=jnp.int32) < count).astype(jnp.float32)
    loss, pull = jax.vjp(lambda e: local_loss(e, positions, live, probe, phase, measured), extended)
    return pull(jnp.ones_like(loss))[0]

def reference(object_slices, probe, phase, positions, counts, measured):
    tiles = object_slices.reshape(SLICES, 2, N_ROW, TILE, N_COL, TILE).transpose(2, 4, 0, 1, 3, 5)
    edge = TILE + WINDOW_PIXELS
    flattened_positions = positions.reshape(N_ROW * N_COL, PROBE_SLOTS, 2)
    flattened_counts = counts.reshape(N_ROW * N_COL)
    flattened_measurements = measured.reshape(N_ROW * N_COL, PROBE_SLOTS, WINDOW_PIXELS, WINDOW_PIXELS)
    for step in range(ITERS):
        right = jnp.roll(tiles, -1, axis=1)[..., :WINDOW_PIXELS]
        wide = jnp.concatenate([tiles, right], axis=-1)
        below = jnp.roll(wide, -1, axis=0)[..., :WINDOW_PIXELS, :]
        extended = jnp.concatenate([wide, below], axis=-2)
        flattened_extended = extended.reshape(N_ROW * N_COL, SLICES, 2, edge, edge)
        gradient_list = lax.map(lambda element: tile_gradient(element[0], element[1], element[2], element[3], probe, phase), (flattened_extended, flattened_positions, flattened_counts, flattened_measurements))
        gradient_list = gradient_list.reshape(N_ROW, N_COL, SLICES, 2, edge, edge)
        bottom = gradient_list[..., TILE:, :]
        upper = gradient_list[..., :TILE, :].at[..., :WINDOW_PIXELS, :].add(jnp.roll(bottom, 1, axis=0))
        side = upper[..., TILE:]
        owned = upper[..., :TILE].at[..., :WINDOW_PIXELS].add(jnp.roll(side, 1, axis=1))
        tiles = tiles - step_rate * owned
    return tiles.transpose(2, 3, 0, 4, 1, 5).reshape(SLICES, 2, N_ROW * TILE, N_COL * TILE)
```

```python
import functools

import jax
import jax.numpy as jnp
import numpy as np
from jax import lax
from jax.experimental import pallas as pl
from jax.experimental.pallas import tpu as pltpu
from jax.sharding import PartitionSpec as P

ITERS = 2
STEP_RATE = 0.02
MESH = pl.DeviceIdType.MESH
N = 128
SLOTS = 4
PAIRS = 2

FR, FB, FD, GD, GB, GR = range(6)
FORWARD, INVERSE = 0, 1


def dft_tables():
    index = np.arange(N)
    angle = (index[:, None] * index[None, :] % N) * (-2.0 * np.pi / N)
    real, imag = np.cos(angle) / np.sqrt(N), np.sin(angle) / np.sqrt(N)
    right = np.block([[real, imag], [-imag, real]]).astype(np.float32)
    rights, lefts = [], []
    for table in (right, right.T):
        high = table.astype(jnp.bfloat16)
        low = (table - high.astype(np.float32)).astype(jnp.bfloat16)
        rights.append(np.concatenate([high, low, high], axis=0))
        lefts.append(np.concatenate([high.T, low.T, high.T], axis=1))
    return np.stack(rights), np.stack(lefts)


def split(value):
    high = value.astype(jnp.bfloat16)
    low = (value - high.astype(jnp.float32)).astype(jnp.bfloat16)
    return high, low


def kernel(
    axes,
    pos_ref,
    count_ref,
    obj_hbm,
    probe_ref,
    phase_ref,
    measured_hbm,
    rights_hbm,
    lefts_hbm,
    out_ref,
    ext0,
    ext1,
    win,
    wave,
    grad,
    in_corner,
    in_bottom,
    in_side,
    pad,
    measured,
    rights,
    lefts,
    prop,
    send_sem,
    recv_sem,
    local_sem,
):
    rows, cols = axes
    row, col = lax.axis_index("row"), lax.axis_index("col")
    left = (row, lax.rem(col + cols - 1, cols))
    right = (row, lax.rem(col + 1, cols))
    above = (lax.rem(row + rows - 1, rows), col)
    below = (lax.rem(row + 1, rows), col)
    exts = (ext0, ext1)

    barrier = pltpu.get_barrier_semaphore()
    for neighbour in (left, right, above, below):
        pl.semaphore_signal(barrier, inc=1, device_id=neighbour, device_id_type=MESH)

    def local(source, target, sem):
        return pltpu.make_async_copy(source, target, local_sem.at[sem])

    own_copies = [local(obj_hbm.at[s], exts[s].at[0, :, 0:N, :], s) for s in range(2)]
    table_copies = [local(rights_hbm, rights, 2), local(lefts_hbm, lefts, 3)]
    measured_copy = local(measured_hbm, measured, 4)
    for copy in own_copies + table_copies + [measured_copy]:
        copy.start()

    def remote(kind, s, source, target, device, c):
        return pltpu.make_async_remote_copy(
            src_ref=source,
            dst_ref=target,
            send_sem=send_sem.at[kind, s, c],
            recv_sem=recv_sem.at[kind, s, c],
            device_id=device,
            device_id_type=MESH,
        )

    def copies(kind, s, first=False):
        made = []
        for c in range(2):
            ext = exts[s]
            own = obj_hbm.at[s, c] if first else ext.at[0, c, 0:N, :]
            side = ext.at[1, c, 0:N, :]
            if kind == FR:
                args = (own, side, left)
            elif kind == FB:
                args = (own, ext.at[0, c, N : 2 * N, :], above)
            elif kind == FD:
                args = (side, ext.at[1, c, N : 2 * N, :], above)
            elif kind == GD:
                args = (grad.at[s, 3, c], in_corner.at[s, c], below)
            elif kind == GB:
                args = (grad.at[s, 2, c], in_bottom.at[s, c], below)
            else:
                args = (grad.at[s, 1, c], in_side.at[s, c], right)
            made.append(remote(kind, s, *args, c))
        return made

    lane = lax.broadcasted_iota(jnp.int32, (N, N), 1)

    def gather(s):
        ext = exts[s]
        for k in range(SLOTS):
            p, q = pos_ref[k, 0], pos_ref[k, 1]
            back = (N - q) & (N - 1)
            for c in range(2):
                near = ext[0, c, pl.ds(p, N), :]
                far = ext[1, c, pl.ds(p, N), :]
                mixed = pltpu.roll(jnp.where(lane >= q, near, far), back, 1)
                win[s, c, k // 2, :, (k % 2) * N : (k % 2 + 1) * N] = mixed

    def scatter_slot(k, c, value):
        q = pos_ref[k, 1]
        moved = pltpu.roll(value, q, 1)
        pad[k, 0, c, N : 2 * N, :] = jnp.where(lane >= q, moved, 0.0)
        pad[k, 1, c, N : 2 * N, :] = jnp.where(lane < q, moved, 0.0)

    def collect(s, quadrant):
        v, h = quadrant // 2, quadrant % 2
        for c in range(2):
            total = pad[0, h, c, pl.ds((v + 1) * N - pos_ref[0, 0], N), :]
            for k in range(1, SLOTS):
                total += pad[k, h, c, pl.ds((v + 1) * N - pos_ref[k, 0], N), :]
            grad[s, quadrant, c] = total

    def columns(re, im, which):
        high, low = split(jnp.concatenate([re, im], axis=0))
        stacked = jnp.concatenate([high, high, low], axis=0)
        out = jnp.dot(lefts[which], stacked, preferred_element_type=jnp.float32)
        return out[:N], out[N:]

    def lines(re, im, which):
        block = jnp.concatenate(
            [
                jnp.concatenate([re[:, :N], im[:, :N]], axis=1),
                jnp.concatenate([re[:, N:], im[:, N:]], axis=1),
            ],
            axis=0,
        )
        high, low = split(block)
        stacked = jnp.concatenate([high, high, low], axis=1)
        out = jnp.dot(stacked, rights[which], preferred_element_type=jnp.float32)
        return (
            jnp.concatenate([out[:N, :N], out[N:, :N]], axis=1),
            jnp.concatenate([out[:N, N:], out[N:, N:]], axis=1),
        )

    def twice(value):
        return jnp.concatenate([value, value], axis=1)

    pl.semaphore_wait(barrier, 4)
    started = {}

    def start(kind, s, first=False):
        started[kind, s] = copies(kind, s, first)
        for copy in started[kind, s]:
            copy.start()

    def wait_send(kind, s):
        for copy in started.pop((kind, s)):
            copy.wait_send()

    for s in range(2):
        start(FR, s, True)
        start(FB, s, True)

    prop[0] = jnp.cos(phase_ref[...])
    prop[1] = jnp.sin(phase_ref[...])
    zero = jnp.zeros((N, N), jnp.float32)
    for k in range(SLOTS):
        for h in range(2):
            for c in range(2):
                pad[k, h, c, 0:N, :] = zero
                pad[k, h, c, 2 * N : 3 * N, :] = zero
    for copy in own_copies + table_copies + [measured_copy]:
        copy.wait()

    def pass_on(s):
        arrived = started[FR, s]
        passed = copies(FD, s)
        for c in range(2):
            arrived[c].wait_recv()
            passed[c].start()
        started[FD, s] = passed

    def wait_recv(kind, s):
        for copy in started[kind, s]:
            copy.wait_recv()

    for step in range(ITERS):
        last = step == ITERS - 1
        order = (0, 1) if step == 0 else (1, 0)
        pass_on(order[0])
        pass_on(order[1])
        wait_recv(FB, 0)
        wait_recv(FD, 0)
        gather(0)

        for pair in range(PAIRS):
            p_re, p_im = twice(probe_ref[0]), twice(probe_ref[1])
            h_re, h_im = twice(prop[0]), twice(prop[1])
            o_re, o_im = win[0, 0, pair], win[0, 1, pair]
            re, im = p_re * o_re - p_im * o_im, p_re * o_im + p_im * o_re
            re, im = lines(re, im, FORWARD)
            re, im = columns(re, im, FORWARD)
            re, im = re * h_re - im * h_im, re * h_im + im * h_re
            re, im = columns(re, im, INVERSE)
            re, im = lines(re, im, INVERSE)
            wave[0, pair] = re
            wave[1, pair] = im

        wait_recv(FB, 1)
        wait_recv(FD, 1)
        gather(1)
        for pair in range(PAIRS):
            w_re, w_im = wave[0, pair], wave[1, pair]
            o_re, o_im = win[1, 0, pair], win[1, 1, pair]
            re, im = w_re * o_re - w_im * o_im, w_re * o_im + w_im * o_re
            re, im = lines(re, im, FORWARD)
            re, im = columns(re, im, FORWARD)
            seen = jnp.concatenate([measured[2 * pair], measured[2 * pair + 1]], axis=1)
            wide = lax.broadcasted_iota(jnp.int32, (N, 2 * N), 1)
            slot = jnp.where(wide < N, 2 * pair, 2 * pair + 1)
            factor = 2.0 * (re * re + im * im - seen)
            factor = jnp.where(slot < count_ref[0], factor, 0.0)
            re, im = columns(re * factor, im * factor, INVERSE)
            re, im = lines(re, im, INVERSE)
            g_re, g_im = w_re * re + w_im * im, w_re * im - w_im * re
            for half in range(2):
                k, part = 2 * pair + half, slice(half * N, (half + 1) * N)
                scatter_slot(k, 0, g_re[:, part])
                scatter_slot(k, 1, g_im[:, part])
            wave[0, pair] = o_re * re + o_im * im
            wave[1, pair] = o_re * im - o_im * re

        def send_back(s):
            for kind in (GD, GB, GR):
                if (kind, s) in started:
                    wait_send(kind, s)
            collect(s, 3)
            start(GD, s)
            collect(s, 2)
            start(GB, s)
            collect(s, 1)
            collect(s, 0)

        def add_corner(s):
            wait_send(FD, s)
            arrived, passed = started[GD, s], copies(GR, s)
            for c in range(2):
                arrived[c].wait_recv()
                grad[s, 1, c] = grad[s, 1, c] + in_corner[s, c]
                passed[c].start()
            started[GR, s] = passed

        def update(s):
            for kind in (FR, FB):
                if (kind, s) in started:
                    wait_send(kind, s)
            wait_recv(GB, s)
            arrived = started[GR, s]
            for c in range(2):
                arrived[c].wait_recv()
                total = grad[s, 0, c] + in_bottom[s, c] + in_side[s, c]
                new = exts[s][0, c, 0:N, :] - STEP_RATE * total
                if last:
                    out_ref[s, c] = new
                else:
                    exts[s][0, c, 0:N, :] = new
            if not last:
                start(FR, s)
                start(FB, s)

        send_back(1)

        def back(pair):
            h_re, h_im = twice(prop[0]), twice(prop[1])
            re, im = wave[0, pair], wave[1, pair]
            re, im = lines(re, im, FORWARD)
            re, im = columns(re, im, FORWARD)
            re, im = h_re * re + h_im * im, h_re * im - h_im * re
            re, im = columns(re, im, INVERSE)
            re, im = lines(re, im, INVERSE)
            p_re, p_im = twice(probe_ref[0]), twice(probe_ref[1])
            g_re, g_im = p_re * re + p_im * im, p_re * im - p_im * re
            for half in range(2):
                k, part = 2 * pair + half, slice(half * N, (half + 1) * N)
                scatter_slot(k, 0, g_re[:, part])
                scatter_slot(k, 1, g_im[:, part])

        back(0)
        add_corner(1)
        back(1)
        send_back(0)
        update(1)
        add_corner(0)
        update(0)

    for kind, s in list(started):
        wait_send(kind, s)


def per_device(object_slices, probe, phase, positions, counts, measured):
    rights, lefts = dft_tables()
    vmem = pl.BlockSpec(memory_space=pltpu.VMEM)
    smem = pl.BlockSpec(memory_space=pltpu.SMEM)
    anywhere = pl.BlockSpec(memory_space=pl.ANY)
    f32 = jnp.float32
    return pl.pallas_call(
        functools.partial(kernel, (lax.axis_size("row"), lax.axis_size("col"))),
        out_shape=jax.ShapeDtypeStruct((2, 2, N, N), f32),
        in_specs=[smem, smem, anywhere, vmem, vmem, anywhere, anywhere, anywhere],
        out_specs=vmem,
        scratch_shapes=[
            pltpu.VMEM((2, 2, 2 * N, N), f32),
            pltpu.VMEM((2, 2, 2 * N, N), f32),
            pltpu.VMEM((2, 2, PAIRS, N, 2 * N), f32),
            pltpu.VMEM((2, PAIRS, N, 2 * N), f32),
            pltpu.VMEM((2, 4, 2, N, N), f32),
            pltpu.VMEM((2, 2, N, N), f32),
            pltpu.VMEM((2, 2, N, N), f32),
            pltpu.VMEM((2, 2, N, N), f32),
            pltpu.VMEM((SLOTS, 2, 2, 3 * N, N), f32),
            pltpu.VMEM((SLOTS, N, N), f32),
            pltpu.VMEM((2, 6 * N, 2 * N), jnp.bfloat16),
            pltpu.VMEM((2, 2 * N, 6 * N), jnp.bfloat16),
            pltpu.VMEM((2, N, N), f32),
            pltpu.SemaphoreType.DMA((6, 2, 2)),
            pltpu.SemaphoreType.DMA((6, 2, 2)),
            pltpu.SemaphoreType.DMA((5,)),
        ],
        compiler_params=pltpu.CompilerParams(
            collective_id=0, has_side_effects=True, vmem_limit_bytes=56 * 1024 * 1024
        ),
        cost_estimate=pl.CostEstimate(
            flops=6 * 805306368, bytes_accessed=2500000, transcendentals=0
        ),
    )(
        positions.reshape(SLOTS, 2),
        counts.reshape(1),
        object_slices,
        probe,
        phase,
        measured.reshape(SLOTS, N, N),
        jnp.asarray(rights),
        jnp.asarray(lefts),
    )


def solution(mesh):
    return jax.shard_map(
        per_device,
        mesh=mesh,
        in_specs=(
            P(None, None, "row", "col"),
            P(),
            P(),
            P("row", "col", None, None),
            P("row", "col"),
            P("row", "col", None, None, None),
        ),
        out_specs=P(None, None, "row", "col"),
        check_vma=False,
    )
```

```python
import functools

import jax
import jax.numpy as jnp
import numpy as np
from jax import lax
from jax.experimental import pallas as pl
from jax.experimental.pallas import tpu as pltpu
from jax.sharding import PartitionSpec as P

ITERS = 2
STEP_RATE = 0.02
MESH = pl.DeviceIdType.MESH
N = 128
SLOTS = 4
PAIRS = 2

FR, FB, FD, GD, GB, GR, FE, GE = range(8)
RUN = 8
FORWARD, INVERSE = 0, 1


def dft_tables():
    index = np.arange(N)
    angle = (index[:, None] * index[None, :] % N) * (-2.0 * np.pi / N)
    real, imag = np.cos(angle) / np.sqrt(N), np.sin(angle) / np.sqrt(N)
    right = np.block([[real, imag], [-imag, real]]).astype(np.float32)
    rights, lefts = [], []
    for table in (right, right.T):
        high = table.astype(jnp.bfloat16)
        low = (table - high.astype(np.float32)).astype(jnp.bfloat16)
        rights.append(np.concatenate([high, low, high], axis=0))
        lefts.append(np.concatenate([high.T, low.T, high.T], axis=1))
    return np.stack(rights), np.stack(lefts)


def split(value):
    high = value.astype(jnp.bfloat16)
    low = (value - high.astype(jnp.float32)).astype(jnp.bfloat16)
    return high, low


def kernel(
    axes,
    pos_hbm,
    count_hbm,
    obj_hbm,
    probe_hbm,
    phase_hbm,
    measured_hbm,
    rights_hbm,
    lefts_hbm,
    out_ref,
    ext0,
    ext1,
    win,
    wave,
    grad,
    in_corner,
    in_bottom,
    in_side,
    in_extra,
    pad,
    positions,
    counts,
    probe_ref,
    phase_ref,
    measured,
    rights,
    lefts,
    prop,
    send_sem,
    recv_sem,
    local_sem,
):
    rows, cols = axes
    row, col = lax.axis_index("row"), lax.axis_index("col")
    left = (row, lax.rem(col + cols - 1, cols))
    right = (row, lax.rem(col + 1, cols))
    above = (lax.rem(row + rows - 1, rows), col)
    below = (lax.rem(row + 1, rows), col)
    exts = (ext0, ext1)

    barrier = pltpu.get_barrier_semaphore()
    for neighbour in (left, right, above, below):
        pl.semaphore_signal(barrier, inc=1, device_id=neighbour, device_id_type=MESH)

    def local(source, target, sem):
        return pltpu.make_async_copy(source, target, local_sem.at[sem])

    small_copies = [
        local(pos_hbm, positions, 5),
        local(count_hbm, counts, 6),
        local(probe_hbm, probe_ref, 7),
        local(phase_hbm, phase_ref, 8),
    ]
    own_copies = [local(obj_hbm.at[s], exts[s].at[0, :, 0:N, :], s) for s in range(2)]
    table_copies = [local(rights_hbm, rights, 2), local(lefts_hbm, lefts, 3)]
    measured_copy = local(measured_hbm, measured, 4)
    argument_copies = small_copies + own_copies + table_copies + [measured_copy]
    for copy in argument_copies:
        copy.start()

    row_end, row_start = lax.rem(row, RUN) == RUN - 1, lax.rem(row, RUN) == 0
    col_end, col_start = lax.rem(col, RUN) == RUN - 1, lax.rem(col, RUN) == 0
    passes_up = jnp.logical_not(row_start & col_end)
    passes_left = row_end & col_start
    corner_down = jnp.logical_not(row_end & col_start)
    corner_right = row_end & col_start
    corner_from_above = jnp.logical_not(row_start & col_start)
    corner_from_left = row_end & (lax.rem(col, RUN) == 1)

    def piece(kind, s, c, first=False):
        ext = exts[s]
        own = obj_hbm.at[s, c] if first else ext.at[0, c, 0:N, :]
        side, bottom = ext.at[1, c, 0:N, :], ext.at[0, c, N : 2 * N, :]
        corner = ext.at[1, c, N : 2 * N, :]
        source, target, device = {
            FR: (own, side, left),
            FB: (own, bottom, above),
            FD: (side, corner, above),
            FE: (bottom, corner, left),
            GD: (grad.at[s, 3, c], in_corner.at[s, c], below),
            GE: (grad.at[s, 3, c], in_extra.at[s, c], right),
            GB: (grad.at[s, 2, c], in_bottom.at[s, c], below),
            GR: (grad.at[s, 1, c], in_side.at[s, c], right),
        }[kind]
        landing = FD if kind == FE else kind
        return pltpu.make_async_remote_copy(
            src_ref=source,
            dst_ref=target,
            send_sem=send_sem.at[kind, s, c],
            recv_sem=recv_sem.at[landing, s, c],
            device_id=device,
            device_id_type=MESH,
        )

    def copies(kind, s, first=False):
        return (piece(kind, s, c, first) for c in range(2))

    lane = lax.broadcasted_iota(jnp.int32, (N, N), 1)

    def gather(s):
        ext = exts[s]
        for k in range(SLOTS):
            p, q = positions[0, 0, 0, k], positions[0, 0, 1, k]
            back = (N - q) & (N - 1)
            for c in range(2):
                near = ext[0, c, pl.ds(p, N), :]
                far = ext[1, c, pl.ds(p, N), :]
                mixed = pltpu.roll(jnp.where(lane >= q, near, far), back, 1)
                win[s, c, k // 2, :, (k % 2) * N : (k % 2 + 1) * N] = mixed

    def scatter_slot(k, c, value):
        q = positions[0, 0, 1, k]
        moved = pltpu.roll(value, q, 1)
        pad[k, 0, c, N : 2 * N, :] = jnp.where(lane >= q, moved, 0.0)
        pad[k, 1, c, N : 2 * N, :] = jnp.where(lane < q, moved, 0.0)

    def collect(s, quadrant):
        v, h = quadrant // 2, quadrant % 2
        for c in range(2):
            total = pad[0, h, c, pl.ds((v + 1) * N - positions[0, 0, 0, 0], N), :]
            for k in range(1, SLOTS):
                total += pad[k, h, c, pl.ds((v + 1) * N - positions[0, 0, 0, k], N), :]
            grad[s, quadrant, c] = total

    def columns(re, im, which):
        high, low = split(jnp.concatenate([re, im], axis=0))
        stacked = jnp.concatenate([high, high, low], axis=0)
        out = jnp.dot(lefts[which], stacked, preferred_element_type=jnp.float32)
        return out[:N], out[N:]

    def lines(re, im, which):
        block = jnp.concatenate(
            [
                jnp.concatenate([re[:, :N], im[:, :N]], axis=1),
                jnp.concatenate([re[:, N:], im[:, N:]], axis=1),
            ],
            axis=0,
        )
        high, low = split(block)
        stacked = jnp.concatenate([high, high, low], axis=1)
        out = jnp.dot(stacked, rights[which], preferred_element_type=jnp.float32)
        return (
            jnp.concatenate([out[:N, :N], out[N:, :N]], axis=1),
            jnp.concatenate([out[:N, N:], out[N:, N:]], axis=1),
        )

    def twice(value):
        return jnp.concatenate([value, value], axis=1)

    pl.semaphore_wait(barrier, 4)
    first_sent = set()

    def start(kind, s, first=False):
        if first:
            first_sent.add((kind, s))
        for copy in copies(kind, s, first):
            copy.start()

    def wait_send(kind, s):
        first = (kind, s) in first_sent
        first_sent.discard((kind, s))
        for copy in copies(kind, s, first):
            copy.wait_send()

    def wait_recv(kind, s):
        for copy in copies(kind, s):
            copy.wait_recv()

    start(FR, 0, True)
    start(FB, 0, True)

    for copy in argument_copies:
        copy.wait()
    prop[0] = jnp.cos(phase_ref[...])
    prop[1] = jnp.sin(phase_ref[...])
    zero = jnp.zeros((N, N), jnp.float32)
    for k in range(SLOTS):
        for h in range(2):
            for c in range(2):
                pad[k, h, c, 0:N, :] = zero
                pad[k, h, c, 2 * N : 3 * N, :] = zero

    wait_send(FB, 0)
    start(FB, 1, True)
    wait_send(FR, 0)
    start(FR, 1, True)

    def pass_on(s):
        for c in range(2):
            piece(FR, s, c).wait_recv()

            @pl.when(passes_up)
            def _():
                piece(FD, s, c).start()

        for c in range(2):
            piece(FB, s, c).wait_recv()

            @pl.when(passes_left)
            def _():
                piece(FE, s, c).start()

    for step in range(ITERS):
        last = step == ITERS - 1
        if step == 0:
            pass_on(0)
            wait_recv(FD, 0)
            gather(0)
            pass_on(1)
        else:
            pass_on(1)
            pass_on(0)
            wait_recv(FD, 0)
            gather(0)

        for pair in range(PAIRS):
            p_re, p_im = twice(probe_ref[0]), twice(probe_ref[1])
            h_re, h_im = twice(prop[0]), twice(prop[1])
            o_re, o_im = win[0, 0, pair], win[0, 1, pair]
            re, im = p_re * o_re - p_im * o_im, p_re * o_im + p_im * o_re
            re, im = lines(re, im, FORWARD)
            re, im = columns(re, im, FORWARD)
            re, im = re * h_re - im * h_im, re * h_im + im * h_re
            re, im = columns(re, im, INVERSE)
            re, im = lines(re, im, INVERSE)
            wave[0, pair] = re
            wave[1, pair] = im

        wait_recv(FD, 1)
        gather(1)
        for pair in range(PAIRS):
            w_re, w_im = wave[0, pair], wave[1, pair]
            o_re, o_im = win[1, 0, pair], win[1, 1, pair]
            re, im = w_re * o_re - w_im * o_im, w_re * o_im + w_im * o_re
            re, im = lines(re, im, FORWARD)
            re, im = columns(re, im, FORWARD)
            seen = jnp.concatenate([measured[2 * pair], measured[2 * pair + 1]], axis=1)
            wide = lax.broadcasted_iota(jnp.int32, (N, 2 * N), 1)
            slot = jnp.where(wide < N, 2 * pair, 2 * pair + 1)
            factor = 2.0 * (re * re + im * im - seen)
            factor = jnp.where(slot < counts[0, 0], factor, 0.0)
            re, im = columns(re * factor, im * factor, INVERSE)
            re, im = lines(re, im, INVERSE)
            g_re, g_im = w_re * re + w_im * im, w_re * im - w_im * re
            for half in range(2):
                k, part = 2 * pair + half, slice(half * N, (half + 1) * N)
                scatter_slot(k, 0, g_re[:, part])
                scatter_slot(k, 1, g_im[:, part])
            wave[0, pair] = o_re * re + o_im * im
            wave[1, pair] = o_re * im - o_im * re

        def send_back(s):
            @pl.when(passes_up)
            def _():
                wait_send(FD, s)

            @pl.when(passes_left)
            def _():
                wait_send(FE, s)

            collect(s, 3)

            @pl.when(corner_down)
            def _():
                start(GD, s)

            @pl.when(corner_right)
            def _():
                start(GE, s)

            collect(s, 2)

            @pl.when(jnp.logical_not(corner_from_left))
            def _():
                start(GB, s)

            collect(s, 1)
            collect(s, 0)

            @pl.when(corner_from_left)
            def _():
                for c in range(2):
                    piece(GE, s, c).wait_recv()
                    grad[s, 2, c] = grad[s, 2, c] + in_extra[s, c]
                    piece(GB, s, c).start()

        def add_corner(s):
            for c in range(2):

                @pl.when(corner_from_above)
                def _():
                    piece(GD, s, c).wait_recv()
                    grad[s, 1, c] = grad[s, 1, c] + in_corner[s, c]

                piece(GR, s, c).start()

        def update(s):
            @pl.when(corner_down)
            def _():
                wait_send(GD, s)

            @pl.when(corner_right)
            def _():
                wait_send(GE, s)

            wait_send(GB, s)
            wait_send(GR, s)
            if step > 0 or s == 1:
                wait_send(FR, s)
                wait_send(FB, s)
            for c in range(2):
                piece(GB, s, c).wait_recv()
                piece(GR, s, c).wait_recv()
                total = grad[s, 0, c] + in_bottom[s, c] + in_side[s, c]
                new = exts[s][0, c, 0:N, :] - STEP_RATE * total
                if last:
                    out_ref[s, c] = new
                else:
                    exts[s][0, c, 0:N, :] = new
            if not last:
                start(FR, s)
                start(FB, s)

        send_back(1)

        def back(pair):
            h_re, h_im = twice(prop[0]), twice(prop[1])
            re, im = wave[0, pair], wave[1, pair]
            re, im = lines(re, im, FORWARD)
            re, im = columns(re, im, FORWARD)
            re, im = h_re * re + h_im * im, h_re * im - h_im * re
            re, im = columns(re, im, INVERSE)
            re, im = lines(re, im, INVERSE)
            p_re, p_im = twice(probe_ref[0]), twice(probe_ref[1])
            g_re, g_im = p_re * re + p_im * im, p_re * im - p_im * re
            for half in range(2):
                k, part = 2 * pair + half, slice(half * N, (half + 1) * N)
                scatter_slot(k, 0, g_re[:, part])
                scatter_slot(k, 1, g_im[:, part])

        back(0)
        add_corner(1)
        back(1)
        send_back(0)
        add_corner(0)
        update(1)
        update(0)


def per_device(object_slices, probe, phase, positions, counts, measured):
    rights, lefts = dft_tables()
    vmem = pl.BlockSpec(memory_space=pltpu.VMEM)
    hbm = pl.BlockSpec(memory_space=pltpu.HBM)
    f32 = jnp.float32
    return pl.pallas_call(
        functools.partial(kernel, (lax.axis_size("row"), lax.axis_size("col"))),
        out_shape=jax.ShapeDtypeStruct((2, 2, N, N), f32),
        in_specs=[hbm] * 8,
        out_specs=vmem,
        scratch_shapes=[
            pltpu.VMEM((2, 2, 2 * N, N), f32),
            pltpu.VMEM((2, 2, 2 * N, N), f32),
            pltpu.VMEM((2, 2, PAIRS, N, 2 * N), f32),
            pltpu.VMEM((2, PAIRS, N, 2 * N), f32),
            pltpu.VMEM((2, 4, 2, N, N), f32),
            pltpu.VMEM((2, 2, N, N), f32),
            pltpu.VMEM((2, 2, N, N), f32),
            pltpu.VMEM((2, 2, N, N), f32),
            pltpu.VMEM((2, 2, N, N), f32),
            pltpu.VMEM((SLOTS, 2, 2, 3 * N, N), f32),
            pltpu.SMEM((1, 1, 2, SLOTS), jnp.int32),
            pltpu.SMEM((1, 1), jnp.int32),
            pltpu.VMEM((2, N, N), f32),
            pltpu.VMEM((N, N), f32),
            pltpu.VMEM((SLOTS, N, N), f32),
            pltpu.VMEM((2, 6 * N, 2 * N), jnp.bfloat16),
            pltpu.VMEM((2, 2 * N, 6 * N), jnp.bfloat16),
            pltpu.VMEM((2, N, N), f32),
            pltpu.SemaphoreType.DMA((8, 2, 2)),
            pltpu.SemaphoreType.DMA((8, 2, 2)),
            pltpu.SemaphoreType.DMA((9,)),
        ],
        compiler_params=pltpu.CompilerParams(
            collective_id=0, has_side_effects=True, vmem_limit_bytes=56 * 1024 * 1024
        ),
        cost_estimate=pl.CostEstimate(
            flops=6 * 805306368, bytes_accessed=2500000, transcendentals=0
        ),
    )(
        positions.transpose(0, 1, 3, 2),
        counts,
        object_slices,
        probe,
        phase,
        measured.reshape(SLOTS, N, N),
        jnp.asarray(rights),
        jnp.asarray(lefts),
    )


def solution(mesh):
    return jax.shard_map(
        per_device,
        mesh=mesh,
        in_specs=(
            P(None, None, "row", "col"),
            P(),
            P(),
            P("row", "col", None, None),
            P("row", "col"),
            P("row", "col", None, None, None),
        ),
        out_specs=P(None, None, "row", "col"),
        check_vma=False,
    )
```

```python
import functools

import jax
import jax.numpy as jnp
import numpy as np
from jax import lax
from jax.experimental import pallas as pl
from jax.experimental.pallas import tpu as pltpu
from jax.sharding import PartitionSpec as P

ITERS = 2
STEP_RATE = 0.02
MESH = pl.DeviceIdType.MESH
N = 128
SLOTS = 4

FR, FB, FD, GD, GB, GR, FE, GE = range(8)
RUN = 8
FORWARD, INVERSE = 0, 1


def dft_tables():
    index = np.arange(N)
    angle = (index[:, None] * index[None, :] % N) * (-2.0 * np.pi / N)
    real, imag = np.cos(angle) / np.sqrt(N), np.sin(angle) / np.sqrt(N)
    right = np.block([[real, imag], [-imag, real]]).astype(np.float32)
    rights, lefts = [], []
    for table in (right, right.T):
        high = table.astype(jnp.bfloat16)
        low = (table - high.astype(np.float32)).astype(jnp.bfloat16)
        rights.append(np.concatenate([high, low, high], axis=0))
        lefts.append(np.concatenate([high.T, low.T, high.T], axis=1))
    return np.stack(rights), np.stack(lefts)


def split(value):
    high = value.astype(jnp.bfloat16)
    low = (value - high.astype(jnp.float32)).astype(jnp.bfloat16)
    return high, low


def kernel(
    axes,
    pos_hbm,
    count_hbm,
    obj_hbm,
    probe_hbm,
    phase_hbm,
    measured_hbm,
    rights_hbm,
    lefts_hbm,
    out_ref,
    ext0,
    ext1,
    win,
    wave,
    grad,
    in_corner,
    in_bottom,
    in_side,
    in_extra,
    in_right,
    partly,
    pad,
    positions,
    counts,
    probe_ref,
    phase_ref,
    measured,
    rights,
    lefts,
    prop,
    send_sem,
    recv_sem,
    local_sem,
):
    rows, cols = axes
    row, col = lax.axis_index("row"), lax.axis_index("col")
    left = (row, lax.rem(col + cols - 1, cols))
    right = (row, lax.rem(col + 1, cols))
    above = (lax.rem(row + rows - 1, rows), col)
    below = (lax.rem(row + 1, rows), col)
    exts = (ext0, ext1)

    barrier = pltpu.get_barrier_semaphore()
    for neighbour in (left, right, above, below):
        pl.semaphore_signal(barrier, inc=1, device_id=neighbour, device_id_type=MESH)

    def local(source, target, sem):
        return pltpu.make_async_copy(source, target, local_sem.at[sem])

    small_copies = [
        local(pos_hbm, positions, 5),
        local(count_hbm, counts, 6),
        local(probe_hbm, probe_ref, 7),
        local(phase_hbm, phase_ref, 8),
    ]
    own_copies = [local(obj_hbm.at[s], exts[s].at[0, :, 0:N, :], s) for s in range(2)]
    table_copies = [local(rights_hbm, rights, 2), local(lefts_hbm, lefts, 3)]
    measured_copy = local(measured_hbm, measured, 4)
    argument_copies = small_copies + own_copies + table_copies + [measured_copy]
    for copy in argument_copies:
        copy.start()

    row_end, row_start = lax.rem(row, RUN) == RUN - 1, lax.rem(row, RUN) == 0
    col_end, col_start = lax.rem(col, RUN) == RUN - 1, lax.rem(col, RUN) == 0
    passes_up = jnp.logical_not(row_start & col_end)
    passes_left = row_end & col_start
    corner_down = jnp.logical_not(row_end & col_start)
    corner_right = row_end & col_start
    corner_from_above = jnp.logical_not(row_start & col_start)
    corner_from_left = row_end & (lax.rem(col, RUN) == 1)

    def piece(step, kind, s, c):
        ext = exts[s]
        side, bottom = ext.at[1, c, 0:N, :], ext.at[0, c, N : 2 * N, :]
        corner, own = ext.at[1, c, N : 2 * N, :], ext.at[0, c, 0:N, :]
        source, target, device = {
            FR: (partly.at[s, c], in_right.at[s, c], left)
            if step
            else (obj_hbm.at[s, c], side, left),
            FB: (own if step else obj_hbm.at[s, c], bottom, above),
            FD: (side, corner, above),
            FE: (bottom, corner, left),
            GD: (grad.at[step, s, 3, c], in_corner.at[step, s, c], below),
            GE: (grad.at[step, s, 3, c], in_extra.at[step, s, c], right),
            GB: (grad.at[step, s, 2, c], in_bottom.at[step, s, c], below),
            GR: (grad.at[step, s, 1, c], in_side.at[step, s, c], right),
        }[kind]
        landing = FD if kind == FE else kind
        return pltpu.make_async_remote_copy(
            src_ref=source,
            dst_ref=target,
            send_sem=send_sem.at[step, kind, s, c],
            recv_sem=recv_sem.at[step, landing, s, c],
            device_id=device,
            device_id_type=MESH,
        )

    def start(step, kind, s):
        for c in range(2):
            piece(step, kind, s, c).start()

    def wait_send(step, kind, s):
        for c in range(2):
            piece(step, kind, s, c).wait_send()

    def wait_recv(step, kind, s):
        for c in range(2):
            piece(step, kind, s, c).wait_recv()

    lane = lax.broadcasted_iota(jnp.int32, (N, N), 1)

    def gather(s):
        ext = exts[s]
        for k in range(SLOTS):
            p, q = positions[0, 0, 0, k], positions[0, 0, 1, k]
            back = (N - q) & (N - 1)
            for c in range(2):
                near = ext[0, c, pl.ds(p, N), :]
                far = ext[1, c, pl.ds(p, N), :]
                mixed = pltpu.roll(jnp.where(lane >= q, near, far), back, 1)
                win[s, c, :, k * N : (k + 1) * N] = mixed

    def scatter_slot(k, c, value):
        q = positions[0, 0, 1, k]
        moved = pltpu.roll(value, q, 1)
        pad[k, 0, c, N : 2 * N, :] = jnp.where(lane >= q, moved, 0.0)
        pad[k, 1, c, N : 2 * N, :] = jnp.where(lane < q, moved, 0.0)

    def collect(step, s, quadrant):
        v, h = quadrant // 2, quadrant % 2
        for c in range(2):
            total = pad[0, h, c, pl.ds((v + 1) * N - positions[0, 0, 0, 0], N), :]
            for k in range(1, SLOTS):
                total += pad[k, h, c, pl.ds((v + 1) * N - positions[0, 0, 0, k], N), :]
            grad[step, s, quadrant, c] = total

    def columns(re, im, which):
        high, low = split(jnp.concatenate([re, im], axis=0))
        stacked = jnp.concatenate([high, high, low], axis=0)
        out = jnp.dot(lefts[which], stacked, preferred_element_type=jnp.float32)
        return out[:N], out[N:]

    def lines(re, im, which):
        block = jnp.concatenate(
            [
                jnp.concatenate([re[:, part], im[:, part]], axis=1)
                for part in (slice(k * N, (k + 1) * N) for k in range(SLOTS))
            ],
            axis=0,
        )
        high, low = split(block)
        stacked = jnp.concatenate([high, high, low], axis=1)
        out = jnp.dot(stacked, rights[which], preferred_element_type=jnp.float32)
        return tuple(
            jnp.concatenate(
                [out[k * N : (k + 1) * N, part] for k in range(SLOTS)], axis=1
            )
            for part in (slice(0, N), slice(N, 2 * N))
        )

    def for_all(value):
        return jnp.concatenate([value] * SLOTS, axis=1)

    def scatter(re, im):
        for k in range(SLOTS):
            scatter_slot(k, 0, re[:, k * N : (k + 1) * N])
            scatter_slot(k, 1, im[:, k * N : (k + 1) * N])

    pl.semaphore_wait(barrier, 4)
    start(0, FR, 0)
    start(0, FB, 0)

    for copy in argument_copies:
        copy.wait()
    prop[0] = jnp.cos(phase_ref[...])
    prop[1] = jnp.sin(phase_ref[...])
    zero = jnp.zeros((N, N), jnp.float32)
    for k in range(SLOTS):
        for h in range(2):
            for c in range(2):
                pad[k, h, c, 0:N, :] = zero
                pad[k, h, c, 2 * N : 3 * N, :] = zero

    wait_send(0, FB, 0)
    start(0, FB, 1)
    wait_send(0, FR, 0)
    start(0, FR, 1)

    def pass_side_up(step, s, c):
        @pl.when(passes_up)
        def _():
            piece(step, FD, s, c).start()

    def take_bottom(step, s):
        for c in range(2):
            piece(step, FB, s, c).wait_recv()

            @pl.when(passes_left)
            def _():
                piece(step, FE, s, c).start()

    def first_halo(s):
        for c in range(2):
            piece(0, FR, s, c).wait_recv()
            pass_side_up(0, s, c)
        take_bottom(0, s)

    def send_back(step, s):
        if step == 0:
            @pl.when(passes_up)
            def _():
                wait_send(0, FD, s)

            @pl.when(passes_left)
            def _():
                wait_send(0, FE, s)

        collect(step, s, 3)

        @pl.when(corner_down)
        def _():
            start(step, GD, s)

        @pl.when(corner_right)
        def _():
            start(step, GE, s)

        collect(step, s, 2)

        @pl.when(jnp.logical_not(corner_from_left))
        def _():
            start(step, GB, s)

        collect(step, s, 1)
        collect(step, s, 0)

        @pl.when(corner_from_left)
        def _():
            for c in range(2):
                piece(step, GE, s, c).wait_recv()
                grad[step, s, 2, c] = grad[step, s, 2, c] + in_extra[step, s, c]
                piece(step, GB, s, c).start()

    def send_side(step, s):
        for c in range(2):

            @pl.when(corner_from_above)
            def _():
                piece(step, GD, s, c).wait_recv()
                grad[step, s, 1, c] = grad[step, s, 1, c] + in_corner[step, s, c]

            piece(step, GR, s, c).start()

    def send_partly(step, s):
        for c in range(2):
            piece(step, GB, s, c).wait_recv()
            total = grad[step, s, 0, c] + in_bottom[step, s, c]
            new = exts[s][0, c, 0:N, :] - STEP_RATE * total
            if step == ITERS - 1:
                out_ref[s, c] = new
            else:
                partly[s, c] = new
                piece(step + 1, FR, s, c).start()

    def finish(step, s):
        for c in range(2):
            piece(step, GR, s, c).wait_recv()
            if step == ITERS - 1:
                out_ref[s, c] = out_ref[s, c] - STEP_RATE * in_side[step, s, c]
            else:
                new = partly[s, c] - STEP_RATE * in_side[step, s, c]
                exts[s][0, c, 0:N, :] = new
                piece(step + 1, FB, s, c).start()
                piece(step + 1, FR, s, c).wait_recv()
                exts[s][1, c, 0:N, :] = in_right[s, c] - STEP_RATE * grad[step, s, 1, c]
                pass_side_up(step + 1, s, c)

    for step in range(ITERS):
        if step == 0:
            first_halo(0)
        else:
            take_bottom(step, 0)
        wait_recv(step, FD, 0)
        gather(0)
        if step == 0:
            first_halo(1)

        p_re, p_im = for_all(probe_ref[0]), for_all(probe_ref[1])
        h_re, h_im = for_all(prop[0]), for_all(prop[1])
        o_re, o_im = win[0, 0], win[0, 1]
        re, im = p_re * o_re - p_im * o_im, p_re * o_im + p_im * o_re
        re, im = lines(re, im, FORWARD)
        re, im = columns(re, im, FORWARD)
        re, im = re * h_re - im * h_im, re * h_im + im * h_re
        re, im = columns(re, im, INVERSE)
        re, im = lines(re, im, INVERSE)
        wave[0] = re
        wave[1] = im

        if step > 0:
            take_bottom(step, 1)
        wait_recv(step, FD, 1)
        gather(1)
        w_re, w_im = wave[0], wave[1]
        o_re, o_im = win[1, 0], win[1, 1]
        re, im = w_re * o_re - w_im * o_im, w_re * o_im + w_im * o_re
        re, im = lines(re, im, FORWARD)
        re, im = columns(re, im, FORWARD)
        seen = jnp.concatenate([measured[k] for k in range(SLOTS)], axis=1)
        slot = lax.broadcasted_iota(jnp.int32, (N, SLOTS * N), 1) // N
        factor = 2.0 * (re * re + im * im - seen)
        factor = jnp.where(slot < counts[0, 0], factor, 0.0)
        re, im = columns(re * factor, im * factor, INVERSE)
        re, im = lines(re, im, INVERSE)
        scatter(w_re * re + w_im * im, w_re * im - w_im * re)
        wave[0] = o_re * re + o_im * im
        wave[1] = o_re * im - o_im * re

        send_back(step, 1)
        re, im = lines(wave[0], wave[1], FORWARD)
        re, im = columns(re, im, FORWARD)
        re, im = h_re * re + h_im * im, h_re * im - h_im * re
        re, im = columns(re, im, INVERSE)
        re, im = lines(re, im, INVERSE)
        send_side(step, 1)
        scatter(p_re * re + p_im * im, p_re * im - p_im * re)
        send_back(step, 0)
        send_partly(step, 1)
        send_side(step, 0)
        send_partly(step, 0)
        finish(step, 1)
        finish(step, 0)

    wait_send(0, FR, 1)
    wait_send(0, FB, 1)
    for step in range(ITERS):
        for s in range(2):

            @pl.when(corner_down)
            def _():
                wait_send(step, GD, s)

            @pl.when(corner_right)
            def _():
                wait_send(step, GE, s)

            wait_send(step, GB, s)
            wait_send(step, GR, s)
            if step > 0:
                wait_send(step, FR, s)
                wait_send(step, FB, s)

                @pl.when(passes_up)
                def _():
                    wait_send(step, FD, s)

                @pl.when(passes_left)
                def _():
                    wait_send(step, FE, s)


def per_device(object_slices, probe, phase, positions, counts, measured):
    rights, lefts = dft_tables()
    vmem = pl.BlockSpec(memory_space=pltpu.VMEM)
    hbm = pl.BlockSpec(memory_space=pltpu.HBM)
    f32 = jnp.float32
    return pl.pallas_call(
        functools.partial(kernel, (lax.axis_size("row"), lax.axis_size("col"))),
        out_shape=jax.ShapeDtypeStruct((2, 2, N, N), f32),
        in_specs=[hbm, pl.BlockSpec(memory_space=pl.ANY)] + [hbm] * 6,
        out_specs=vmem,
        scratch_shapes=[
            pltpu.VMEM((2, 2, 2 * N, N), f32),
            pltpu.VMEM((2, 2, 2 * N, N), f32),
            pltpu.VMEM((2, 2, N, SLOTS * N), f32),
            pltpu.VMEM((2, N, SLOTS * N), f32),
            pltpu.VMEM((ITERS, 2, 4, 2, N, N), f32),
            pltpu.VMEM((ITERS, 2, 2, N, N), f32),
            pltpu.VMEM((ITERS, 2, 2, N, N), f32),
            pltpu.VMEM((ITERS, 2, 2, N, N), f32),
            pltpu.VMEM((ITERS, 2, 2, N, N), f32),
            pltpu.VMEM((2, 2, N, N), f32),
            pltpu.VMEM((2, 2, N, N), f32),
            pltpu.VMEM((SLOTS, 2, 2, 3 * N, N), f32),
            pltpu.SMEM((1, 1, 2, SLOTS), jnp.int32),
            pltpu.SMEM((1, 1), jnp.int32),
            pltpu.VMEM((2, N, N), f32),
            pltpu.VMEM((N, N), f32),
            pltpu.VMEM((SLOTS, N, N), f32),
            pltpu.VMEM((2, 6 * N, 2 * N), jnp.bfloat16),
            pltpu.VMEM((2, 2 * N, 6 * N), jnp.bfloat16),
            pltpu.VMEM((2, N, N), f32),
            pltpu.SemaphoreType.DMA((ITERS, 8, 2, 2)),
            pltpu.SemaphoreType.DMA((ITERS, 8, 2, 2)),
            pltpu.SemaphoreType.DMA((9,)),
        ],
        compiler_params=pltpu.CompilerParams(
            collective_id=0, has_side_effects=True, vmem_limit_bytes=56 * 1024 * 1024
        ),
        cost_estimate=pl.CostEstimate(
            flops=6 * 805306368, bytes_accessed=2500000, transcendentals=0
        ),
    )(
        positions.transpose(0, 1, 3, 2),
        counts,
        object_slices,
        probe,
        phase,
        measured.reshape(SLOTS, N, N),
        jnp.asarray(rights),
        jnp.asarray(lefts),
    )


def solution(mesh):
    return jax.shard_map(
        per_device,
        mesh=mesh,
        in_specs=(
            P(None, None, "row", "col"),
            P(),
            P(),
            P("row", "col", None, None),
            P("row", "col"),
            P("row", "col", None, None, None),
        ),
        out_specs=P(None, None, "row", "col"),
        check_vma=False,
    )
```

```python
import functools

import jax
import jax.numpy as jnp
import numpy as np
from jax import lax
from jax.experimental import pallas as pl
from jax.experimental.pallas import tpu as pltpu
from jax.sharding import PartitionSpec as P

ITERS = 2
STEP_RATE = 0.02
MESH = pl.DeviceIdType.MESH
N = 128
SLOTS = 4

FR, FB, FD, GD, GB, GR, FE, GE, FX, GX = range(10)
RUN = 8
FORWARD, INVERSE = 0, 1


def dft_tables():
    index = np.arange(N)
    angle = (index[:, None] * index[None, :] % N) * (-2.0 * np.pi / N)
    real, imag = np.cos(angle) / np.sqrt(N), np.sin(angle) / np.sqrt(N)
    right = np.block([[real, imag], [-imag, real]]).astype(np.float32)
    rights, lefts = [], []
    for table in (right, right.T):
        high = table.astype(jnp.bfloat16)
        low = (table - high.astype(np.float32)).astype(jnp.bfloat16)
        rights.append(np.concatenate([high, low, high], axis=0))
        lefts.append(np.concatenate([high.T, low.T, high.T], axis=1))
    return np.stack(rights), np.stack(lefts)


def split(value):
    high = value.astype(jnp.bfloat16)
    low = (value - high.astype(jnp.float32)).astype(jnp.bfloat16)
    return high, low


def kernel(
    axes,
    pos_hbm,
    count_hbm,
    obj_hbm,
    probe_hbm,
    phase_hbm,
    measured_hbm,
    rights_hbm,
    lefts_hbm,
    out_ref,
    ext0,
    ext1,
    win,
    wave,
    grad,
    in_corner,
    in_bottom,
    in_side,
    in_extra,
    in_right,
    partly,
    pad,
    positions,
    counts,
    probe_ref,
    phase_ref,
    measured,
    rights,
    lefts,
    prop,
    send_sem,
    recv_sem,
    local_sem,
):
    rows, cols = axes
    row, col = lax.axis_index("row"), lax.axis_index("col")
    left = (row, lax.rem(col + cols - 1, cols))
    right = (row, lax.rem(col + 1, cols))
    above = (lax.rem(row + rows - 1, rows), col)
    below = (lax.rem(row + 1, rows), col)
    above_left, below_right = (above[0], left[1]), (below[0], right[1])
    exts = (ext0, ext1)

    row_end, row_start = lax.rem(row, RUN) == RUN - 1, lax.rem(row, RUN) == 0
    col_end, col_start = lax.rem(col, RUN) == RUN - 1, lax.rem(col, RUN) == 0
    col_edge = col_end | col_start
    passes_up = jnp.logical_not(row_start & col_edge)
    passes_left = row_end & (lax.rem(col, RUN) == 1)
    sends_diagonal = row_start & col_start
    corner_down = jnp.logical_not(row_end & col_edge)
    corner_right = row_end & col_start
    corner_diagonal = row_end & col_end
    corner_from_above = passes_up
    corner_from_left = passes_left
    corner_from_diagonal = sends_diagonal

    barrier = pltpu.get_barrier_semaphore()
    for neighbour in (left, right, above, below):
        pl.semaphore_signal(barrier, inc=1, device_id=neighbour, device_id_type=MESH)
    for takes_part, neighbour in (
        (sends_diagonal, above_left),
        (corner_diagonal, below_right),
    ):

        @pl.when(takes_part)
        def _():
            pl.semaphore_signal(
                barrier, inc=1, device_id=neighbour, device_id_type=MESH
            )


    def local(source, target, sem):
        return pltpu.make_async_copy(source, target, local_sem.at[sem])

    small_copies = [
        local(pos_hbm, positions, 5),
        local(count_hbm, counts, 6),
        local(probe_hbm, probe_ref, 7),
        local(phase_hbm, phase_ref, 8),
    ]
    own_copies = [local(obj_hbm.at[s], exts[s].at[0, :, 0:N, :], s) for s in range(2)]
    table_copies = [local(rights_hbm, rights, 2), local(lefts_hbm, lefts, 3)]
    measured_copy = local(measured_hbm, measured, 4)
    argument_copies = small_copies + own_copies + table_copies + [measured_copy]
    for copy in argument_copies:
        copy.start()

    def piece(step, kind, s, c):
        ext = exts[s]
        side, bottom = ext.at[1, c, 0:N, :], ext.at[0, c, N : 2 * N, :]
        corner, own = ext.at[1, c, N : 2 * N, :], ext.at[0, c, 0:N, :]
        source, target, device = {
            FR: (partly.at[s, c], in_right.at[s, c], left)
            if step
            else (obj_hbm.at[s, c], side, left),
            FB: (own if step else obj_hbm.at[s, c], bottom, above),
            FD: (side, corner, above),
            FE: (bottom, corner, left),
            GD: (grad.at[step, s, 3, c], in_corner.at[step, s, c], below),
            FX: (own if step else obj_hbm.at[s, c], corner, above_left),
            GX: (grad.at[step, s, 3, c], in_extra.at[step, s, c], below_right),
            GE: (grad.at[step, s, 3, c], in_extra.at[step, s, c], right),
            GB: (grad.at[step, s, 2, c], in_bottom.at[step, s, c], below),
            GR: (grad.at[step, s, 1, c], in_side.at[step, s, c], right),
        }[kind]
        landing = {FE: FD, FX: FD, GX: GE}.get(kind, kind)
        return pltpu.make_async_remote_copy(
            src_ref=source,
            dst_ref=target,
            send_sem=send_sem.at[step, kind, s, c],
            recv_sem=recv_sem.at[step, landing, s, c],
            device_id=device,
            device_id_type=MESH,
        )

    def start(step, kind, s):
        for c in range(2):
            piece(step, kind, s, c).start()

    def wait_send(step, kind, s):
        for c in range(2):
            piece(step, kind, s, c).wait_send()

    def wait_recv(step, kind, s):
        for c in range(2):
            piece(step, kind, s, c).wait_recv()

    lane = lax.broadcasted_iota(jnp.int32, (N, N), 1)

    def gather(s):
        ext = exts[s]
        for k in range(SLOTS):
            p, q = positions[0, 0, 0, k], positions[0, 0, 1, k]
            back = (N - q) & (N - 1)
            for c in range(2):
                near = ext[0, c, pl.ds(p, N), :]
                far = ext[1, c, pl.ds(p, N), :]
                mixed = pltpu.roll(jnp.where(lane >= q, near, far), back, 1)
                win[s, c, :, k * N : (k + 1) * N] = mixed

    def scatter_slot(k, c, value):
        q = positions[0, 0, 1, k]
        moved = pltpu.roll(value, q, 1)
        pad[k, 0, c, N : 2 * N, :] = jnp.where(lane >= q, moved, 0.0)
        pad[k, 1, c, N : 2 * N, :] = jnp.where(lane < q, moved, 0.0)

    def collect(step, s, quadrant):
        v, h = quadrant // 2, quadrant % 2
        for c in range(2):
            total = pad[0, h, c, pl.ds((v + 1) * N - positions[0, 0, 0, 0], N), :]
            for k in range(1, SLOTS):
                total += pad[k, h, c, pl.ds((v + 1) * N - positions[0, 0, 0, k], N), :]
            grad[step, s, quadrant, c] = total

    def columns(re, im, which):
        high, low = split(jnp.concatenate([re, im], axis=0))
        stacked = jnp.concatenate([high, high, low], axis=0)
        out = jnp.dot(lefts[which], stacked, preferred_element_type=jnp.float32)
        return out[:N], out[N:]

    def lines(re, im, which):
        block = jnp.concatenate(
            [
                jnp.concatenate([re[:, part], im[:, part]], axis=1)
                for part in (slice(k * N, (k + 1) * N) for k in range(SLOTS))
            ],
            axis=0,
        )
        high, low = split(block)
        stacked = jnp.concatenate([high, high, low], axis=1)
        out = jnp.dot(stacked, rights[which], preferred_element_type=jnp.float32)
        return tuple(
            jnp.concatenate(
                [out[k * N : (k + 1) * N, part] for k in range(SLOTS)], axis=1
            )
            for part in (slice(0, N), slice(N, 2 * N))
        )

    def for_all(value):
        return jnp.concatenate([value] * SLOTS, axis=1)

    def scatter(re, im):
        for k in range(SLOTS):
            scatter_slot(k, 0, re[:, k * N : (k + 1) * N])
            scatter_slot(k, 1, im[:, k * N : (k + 1) * N])

    pl.semaphore_wait(barrier, jnp.where(sends_diagonal | corner_diagonal, 5, 4))

    def send_diagonal(step, s):
        @pl.when(sends_diagonal)
        def _():
            start(step, FX, s)

    start(0, FR, 0)
    start(0, FB, 0)
    send_diagonal(0, 0)

    for copy in argument_copies:
        copy.wait()
    prop[0] = jnp.cos(phase_ref[...])
    prop[1] = jnp.sin(phase_ref[...])
    zero = jnp.zeros((N, N), jnp.float32)
    for k in range(SLOTS):
        for h in range(2):
            for c in range(2):
                pad[k, h, c, 0:N, :] = zero
                pad[k, h, c, 2 * N : 3 * N, :] = zero

    wait_send(0, FB, 0)
    start(0, FB, 1)
    wait_send(0, FR, 0)
    start(0, FR, 1)
    send_diagonal(0, 1)

    def pass_side_up(step, s, c):
        @pl.when(passes_up)
        def _():
            piece(step, FD, s, c).start()

    def take_bottom(step, s):
        for c in range(2):
            piece(step, FB, s, c).wait_recv()

            @pl.when(passes_left)
            def _():
                piece(step, FE, s, c).start()

    def first_halo(s):
        for c in range(2):
            piece(0, FR, s, c).wait_recv()
            pass_side_up(0, s, c)
        take_bottom(0, s)

    def send_back(step, s):
        if step == 0:
            @pl.when(passes_up)
            def _():
                wait_send(0, FD, s)

            @pl.when(passes_left)
            def _():
                wait_send(0, FE, s)

        collect(step, s, 3)

        @pl.when(corner_down)
        def _():
            start(step, GD, s)

        @pl.when(corner_right)
        def _():
            start(step, GE, s)

        @pl.when(corner_diagonal)
        def _():
            start(step, GX, s)

        collect(step, s, 2)

        @pl.when(jnp.logical_not(corner_from_left))
        def _():
            start(step, GB, s)

        collect(step, s, 1)
        collect(step, s, 0)

        @pl.when(corner_from_left)
        def _():
            for c in range(2):
                piece(step, GE, s, c).wait_recv()
                grad[step, s, 2, c] = grad[step, s, 2, c] + in_extra[step, s, c]
                piece(step, GB, s, c).start()

    def send_side(step, s):
        for c in range(2):

            @pl.when(corner_from_above)
            def _():
                piece(step, GD, s, c).wait_recv()
                grad[step, s, 1, c] = grad[step, s, 1, c] + in_corner[step, s, c]

            piece(step, GR, s, c).start()

    def send_partly(step, s):
        for c in range(2):
            @pl.when(corner_from_diagonal)
            def _():
                piece(step, GX, s, c).wait_recv()
                grad[step, s, 0, c] = grad[step, s, 0, c] + in_extra[step, s, c]

            piece(step, GB, s, c).wait_recv()
            total = grad[step, s, 0, c] + in_bottom[step, s, c]
            new = exts[s][0, c, 0:N, :] - STEP_RATE * total
            if step == ITERS - 1:
                out_ref[s, c] = new
            else:
                partly[s, c] = new
                piece(step + 1, FR, s, c).start()

    def finish(step, s):
        for c in range(2):
            piece(step, GR, s, c).wait_recv()
            if step == ITERS - 1:
                out_ref[s, c] = out_ref[s, c] - STEP_RATE * in_side[step, s, c]
            else:
                new = partly[s, c] - STEP_RATE * in_side[step, s, c]
                exts[s][0, c, 0:N, :] = new
                piece(step + 1, FB, s, c).start()

                @pl.when(sends_diagonal)
                def _():
                    piece(step + 1, FX, s, c).start()

                piece(step + 1, FR, s, c).wait_recv()
                exts[s][1, c, 0:N, :] = in_right[s, c] - STEP_RATE * grad[step, s, 1, c]
                pass_side_up(step + 1, s, c)

    for step in range(ITERS):
        if step == 0:
            first_halo(0)
        else:
            take_bottom(step, 0)
        wait_recv(step, FD, 0)
        gather(0)
        if step == 0:
            first_halo(1)

        p_re, p_im = for_all(probe_ref[0]), for_all(probe_ref[1])
        h_re, h_im = for_all(prop[0]), for_all(prop[1])
        o_re, o_im = win[0, 0], win[0, 1]
        re, im = p_re * o_re - p_im * o_im, p_re * o_im + p_im * o_re
        re, im = lines(re, im, FORWARD)
        re, im = columns(re, im, FORWARD)
        re, im = re * h_re - im * h_im, re * h_im + im * h_re
        re, im = columns(re, im, INVERSE)
        re, im = lines(re, im, INVERSE)
        wave[0] = re
        wave[1] = im

        if step > 0:
            take_bottom(step, 1)
        wait_recv(step, FD, 1)
        gather(1)
        w_re, w_im = wave[0], wave[1]
        o_re, o_im = win[1, 0], win[1, 1]
        re, im = w_re * o_re - w_im * o_im, w_re * o_im + w_im * o_re
        re, im = lines(re, im, FORWARD)
        re, im = columns(re, im, FORWARD)
        seen = jnp.concatenate([measured[k] for k in range(SLOTS)], axis=1)
        slot = lax.broadcasted_iota(jnp.int32, (N, SLOTS * N), 1) // N
        factor = 2.0 * (re * re + im * im - seen)
        factor = jnp.where(slot < counts[0, 0], factor, 0.0)
        re, im = columns(re * factor, im * factor, INVERSE)
        re, im = lines(re, im, INVERSE)
        scatter(w_re * re + w_im * im, w_re * im - w_im * re)
        wave[0] = o_re * re + o_im * im
        wave[1] = o_re * im - o_im * re

        send_back(step, 1)
        re, im = lines(wave[0], wave[1], FORWARD)
        re, im = columns(re, im, FORWARD)
        re, im = h_re * re + h_im * im, h_re * im - h_im * re
        re, im = columns(re, im, INVERSE)
        re, im = lines(re, im, INVERSE)
        send_side(step, 1)
        scatter(p_re * re + p_im * im, p_re * im - p_im * re)
        send_back(step, 0)
        send_partly(step, 1)
        send_side(step, 0)
        send_partly(step, 0)
        finish(step, 1)
        finish(step, 0)

    wait_send(0, FR, 1)
    wait_send(0, FB, 1)
    for step in range(ITERS):
        for s in range(2):

            @pl.when(corner_down)
            def _():
                wait_send(step, GD, s)

            @pl.when(corner_right)
            def _():
                wait_send(step, GE, s)

            @pl.when(corner_diagonal)
            def _():
                wait_send(step, GX, s)

            @pl.when(sends_diagonal)
            def _():
                wait_send(step, FX, s)

            wait_send(step, GB, s)
            wait_send(step, GR, s)
            if step > 0:
                wait_send(step, FR, s)
                wait_send(step, FB, s)

                @pl.when(passes_up)
                def _():
                    wait_send(step, FD, s)

                @pl.when(passes_left)
                def _():
                    wait_send(step, FE, s)


def per_device(object_slices, probe, phase, positions, counts, measured):
    rights, lefts = dft_tables()
    vmem = pl.BlockSpec(memory_space=pltpu.VMEM)
    hbm = pl.BlockSpec(memory_space=pltpu.HBM)
    f32 = jnp.float32
    return pl.pallas_call(
        functools.partial(kernel, (lax.axis_size("row"), lax.axis_size("col"))),
        out_shape=jax.ShapeDtypeStruct((2, 2, N, N), f32),
        in_specs=[hbm, pl.BlockSpec(memory_space=pl.ANY)] + [hbm] * 6,
        out_specs=vmem,
        scratch_shapes=[
            pltpu.VMEM((2, 2, 2 * N, N), f32),
            pltpu.VMEM((2, 2, 2 * N, N), f32),
            pltpu.VMEM((2, 2, N, SLOTS * N), f32),
            pltpu.VMEM((2, N, SLOTS * N), f32),
            pltpu.VMEM((ITERS, 2, 4, 2, N, N), f32),
            pltpu.VMEM((ITERS, 2, 2, N, N), f32),
            pltpu.VMEM((ITERS, 2, 2, N, N), f32),
            pltpu.VMEM((ITERS, 2, 2, N, N), f32),
            pltpu.VMEM((ITERS, 2, 2, N, N), f32),
            pltpu.VMEM((2, 2, N, N), f32),
            pltpu.VMEM((2, 2, N, N), f32),
            pltpu.VMEM((SLOTS, 2, 2, 3 * N, N), f32),
            pltpu.SMEM((1, 1, 2, SLOTS), jnp.int32),
            pltpu.SMEM((1, 1), jnp.int32),
            pltpu.VMEM((2, N, N), f32),
            pltpu.VMEM((N, N), f32),
            pltpu.VMEM((SLOTS, N, N), f32),
            pltpu.VMEM((2, 6 * N, 2 * N), jnp.bfloat16),
            pltpu.VMEM((2, 2 * N, 6 * N), jnp.bfloat16),
            pltpu.VMEM((2, N, N), f32),
            pltpu.SemaphoreType.DMA((ITERS, 10, 2, 2)),
            pltpu.SemaphoreType.DMA((ITERS, 10, 2, 2)),
            pltpu.SemaphoreType.DMA((9,)),
        ],
        compiler_params=pltpu.CompilerParams(
            collective_id=0, has_side_effects=True, vmem_limit_bytes=56 * 1024 * 1024
        ),
        cost_estimate=pl.CostEstimate(
            flops=6 * 805306368, bytes_accessed=2500000, transcendentals=0
        ),
    )(
        positions.transpose(0, 1, 3, 2),
        counts,
        object_slices,
        probe,
        phase,
        measured.reshape(SLOTS, N, N),
        jnp.asarray(rights),
        jnp.asarray(lefts),
    )


def solution(mesh):
    return jax.shard_map(
        per_device,
        mesh=mesh,
        in_specs=(
            P(None, None, "row", "col"),
            P(),
            P(),
            P("row", "col", None, None),
            P("row", "col"),
            P("row", "col", None, None, None),
        ),
        out_specs=P(None, None, "row", "col"),
        check_vma=False,
    )
```

```python
import functools

import jax
import jax.numpy as jnp
import numpy as np
from jax import lax
from jax.experimental import pallas as pl
from jax.experimental.pallas import tpu as pltpu
from jax.sharding import PartitionSpec as P

ITERS = 2
STEP_RATE = 0.02
MESH = pl.DeviceIdType.MESH
N = 128
SLOTS = 4

FR, FB, FD, GD, GB, GR, FE, GE, FX, GX = range(10)
DETOUR = (1,)
RUN = 8
FORWARD, INVERSE = 0, 1


def dft_tables():
    index = np.arange(N)
    angle = (index[:, None] * index[None, :] % N) * (-2.0 * np.pi / N)
    real, imag = np.cos(angle) / np.sqrt(N), np.sin(angle) / np.sqrt(N)
    right = np.block([[real, imag], [-imag, real]]).astype(np.float32)
    rights, lefts = [], []
    for table in (right, right.T):
        high = table.astype(jnp.bfloat16)
        low = (table - high.astype(np.float32)).astype(jnp.bfloat16)
        rights.append(np.concatenate([high, low, high], axis=0))
        lefts.append(np.concatenate([high.T, low.T, high.T], axis=1))
    return np.stack(rights), np.stack(lefts)


def split(value):
    high = value.astype(jnp.bfloat16)
    low = (value - high.astype(jnp.float32)).astype(jnp.bfloat16)
    return high, low


def kernel(
    axes,
    pos_hbm,
    count_hbm,
    obj_hbm,
    probe_hbm,
    phase_hbm,
    measured_hbm,
    rights_hbm,
    lefts_hbm,
    out_ref,
    ext0,
    ext1,
    win,
    wave,
    grad,
    in_corner,
    in_bottom,
    in_side,
    in_extra,
    in_right,
    partly,
    pad,
    positions,
    counts,
    probe_ref,
    phase_ref,
    measured,
    rights,
    lefts,
    prop,
    send_sem,
    recv_sem,
    local_sem,
):
    rows, cols = axes
    row, col = lax.axis_index("row"), lax.axis_index("col")
    left = (row, lax.rem(col + cols - 1, cols))
    right = (row, lax.rem(col + 1, cols))
    above = (lax.rem(row + rows - 1, rows), col)
    below = (lax.rem(row + 1, rows), col)
    above_left, below_right = (above[0], left[1]), (below[0], right[1])
    exts = (ext0, ext1)

    row_end, row_start = lax.rem(row, RUN) == RUN - 1, lax.rem(row, RUN) == 0
    col_end, col_start = lax.rem(col, RUN) == RUN - 1, lax.rem(col, RUN) == 0
    next_col = lax.rem(col, RUN) == 1
    sends_diagonal = row_start & col_start
    corner_diagonal = row_end & col_end

    def turns(step, s):
        return step > 0 and s in DETOUR

    def passes_up(step, s):
        return jnp.logical_not(
            row_start & (col_end | col_start if turns(step, s) else col_end)
        )

    def corner_edge(s):
        return col_end | col_start if s in DETOUR else col_end

    barrier = pltpu.get_barrier_semaphore()
    for neighbour in (left, right, above, below):
        pl.semaphore_signal(barrier, inc=1, device_id=neighbour, device_id_type=MESH)
    for takes_part, neighbour in (
        (sends_diagonal, above_left),
        (corner_diagonal, below_right),
    ):

        @pl.when(takes_part)
        def _():
            pl.semaphore_signal(
                barrier, inc=1, device_id=neighbour, device_id_type=MESH
            )


    def local(source, target, sem):
        return pltpu.make_async_copy(source, target, local_sem.at[sem])

    small_copies = [
        local(pos_hbm, positions, 5),
        local(count_hbm, counts, 6),
        local(probe_hbm, probe_ref, 7),
        local(phase_hbm, phase_ref, 8),
    ]
    own_copies = [local(obj_hbm.at[s], exts[s].at[0, :, 0:N, :], s) for s in range(2)]
    table_copies = [local(rights_hbm, rights, 2), local(lefts_hbm, lefts, 3)]
    measured_copy = local(measured_hbm, measured, 4)
    argument_copies = small_copies + own_copies + table_copies + [measured_copy]
    for copy in argument_copies:
        copy.start()

    def piece(step, kind, s, c):
        ext = exts[s]
        side, bottom = ext.at[1, c, 0:N, :], ext.at[0, c, N : 2 * N, :]
        corner, own = ext.at[1, c, N : 2 * N, :], ext.at[0, c, 0:N, :]
        source, target, device = {
            FR: (partly.at[s, c], in_right.at[s, c], left)
            if step
            else (obj_hbm.at[s, c], side, left),
            FB: (own if step else obj_hbm.at[s, c], bottom, above),
            FD: (side, corner, above),
            FE: (bottom, corner, left),
            GD: (grad.at[step, s, 3, c], in_corner.at[step, s, c], below),
            FX: (own if step else obj_hbm.at[s, c], corner, above_left),
            GX: (grad.at[step, s, 3, c], in_extra.at[step, s, c], below_right),
            GE: (grad.at[step, s, 3, c], in_extra.at[step, s, c], right),
            GB: (grad.at[step, s, 2, c], in_bottom.at[step, s, c], below),
            GR: (grad.at[step, s, 1, c], in_side.at[step, s, c], right),
        }[kind]
        landing = {FE: FD, FX: FD, GX: GE}.get(kind, kind)
        return pltpu.make_async_remote_copy(
            src_ref=source,
            dst_ref=target,
            send_sem=send_sem.at[step, kind, s, c],
            recv_sem=recv_sem.at[step, landing, s, c],
            device_id=device,
            device_id_type=MESH,
        )

    def start(step, kind, s):
        for c in range(2):
            piece(step, kind, s, c).start()

    def wait_send(step, kind, s):
        for c in range(2):
            piece(step, kind, s, c).wait_send()

    def wait_recv(step, kind, s):
        for c in range(2):
            piece(step, kind, s, c).wait_recv()

    lane = lax.broadcasted_iota(jnp.int32, (N, N), 1)

    def gather(s):
        ext = exts[s]
        for k in range(SLOTS):
            p, q = positions[0, 0, 0, k], positions[0, 0, 1, k]
            back = (N - q) & (N - 1)
            for c in range(2):
                near = ext[0, c, pl.ds(p, N), :]
                far = ext[1, c, pl.ds(p, N), :]
                mixed = pltpu.roll(jnp.where(lane >= q, near, far), back, 1)
                win[s, c, :, k * N : (k + 1) * N] = mixed

    def scatter_slot(k, c, value):
        pad[k, c, N : 2 * N, :] = pltpu.roll(value, positions[0, 0, 1, k], 1)

    def collect(step, s, v):
        for c in range(2):
            near = far = None
            for k in range(SLOTS):
                q = positions[0, 0, 1, k]
                moved = pad[k, c, pl.ds((v + 1) * N - positions[0, 0, 0, k], N), :]
                first = jnp.where(lane >= q, moved, 0.0)
                second = jnp.where(lane < q, moved, 0.0)
                near = first if near is None else near + first
                far = second if far is None else far + second
            grad[step, s, 2 * v, c] = near
            grad[step, s, 2 * v + 1, c] = far

    def columns(re, im, which):
        high, low = split(jnp.concatenate([re, im], axis=0))
        stacked = jnp.concatenate([high, high, low], axis=0)
        out = jnp.dot(lefts[which], stacked, preferred_element_type=jnp.float32)
        return out[:N], out[N:]

    def lines(re, im, which):
        block = jnp.concatenate(
            [
                jnp.concatenate([re[:, part], im[:, part]], axis=1)
                for part in (slice(k * N, (k + 1) * N) for k in range(SLOTS))
            ],
            axis=0,
        )
        high, low = split(block)
        stacked = jnp.concatenate([high, high, low], axis=1)
        out = jnp.dot(stacked, rights[which], preferred_element_type=jnp.float32)
        return tuple(
            jnp.concatenate(
                [out[k * N : (k + 1) * N, part] for k in range(SLOTS)], axis=1
            )
            for part in (slice(0, N), slice(N, 2 * N))
        )

    def for_all(value):
        return jnp.concatenate([value] * SLOTS, axis=1)

    def scatter(re, im):
        for k in range(SLOTS):
            scatter_slot(k, 0, re[:, k * N : (k + 1) * N])
            scatter_slot(k, 1, im[:, k * N : (k + 1) * N])

    pl.semaphore_wait(barrier, jnp.where(sends_diagonal | corner_diagonal, 5, 4))

    def send_diagonal(step, s):
        @pl.when(sends_diagonal)
        def _():
            start(step, FX, s)

    start(0, FR, 0)
    start(0, FB, 0)
    send_diagonal(0, 0)
    start(0, FR, 1)
    start(0, FB, 1)
    send_diagonal(0, 1)

    for copy in argument_copies:
        copy.wait()
    prop[0] = jnp.cos(phase_ref[...])
    prop[1] = jnp.sin(phase_ref[...])
    zero = jnp.zeros((N, N), jnp.float32)
    for k in range(SLOTS):
        for c in range(2):
            pad[k, c, 0:N, :] = zero
            pad[k, c, 2 * N : 3 * N, :] = zero

    wait_send(0, FB, 0)
    wait_send(0, FR, 0)

    def pass_side_up(step, s, c):
        @pl.when(passes_up(step, s))
        def _():
            piece(step, FD, s, c).start()

    def take_bottom(step, s):
        for c in range(2):
            piece(step, FB, s, c).wait_recv()
            if turns(step, s):

                @pl.when(row_end & next_col)
                def _():
                    piece(step, FE, s, c).start()

    def first_halo(s):
        for c in range(2):
            piece(0, FR, s, c).wait_recv()
            pass_side_up(0, s, c)
        take_bottom(0, s)

    def send_back(step, s):
        if step == 0:
            @pl.when(passes_up(0, s))
            def _():
                wait_send(0, FD, s)

        collect(step, s, 1)

        @pl.when(jnp.logical_not(row_end & corner_edge(s)))
        def _():
            start(step, GD, s)

        @pl.when(corner_diagonal)
        def _():
            start(step, GX, s)

        if s in DETOUR:

            @pl.when(row_end & col_start)
            def _():
                start(step, GE, s)

        if s in DETOUR:

            @pl.when(jnp.logical_not(row_end & next_col))
            def _():
                start(step, GB, s)

        else:
            start(step, GB, s)
        collect(step, s, 0)

    def send_turned(step, s):
        if s in DETOUR:

            @pl.when(row_end & next_col)
            def _():
                for c in range(2):
                    piece(step, GE, s, c).wait_recv()
                    grad[step, s, 2, c] = grad[step, s, 2, c] + in_extra[step, s, c]
                    piece(step, GB, s, c).start()

    def send_side(step, s):
        for c in range(2):

            @pl.when(jnp.logical_not(row_start & corner_edge(s)))
            def _():
                piece(step, GD, s, c).wait_recv()
                grad[step, s, 1, c] = grad[step, s, 1, c] + in_corner[step, s, c]

            piece(step, GR, s, c).start()

    def send_partly(step, s):
        for c in range(2):
            @pl.when(sends_diagonal)
            def _():
                piece(step, GX, s, c).wait_recv()
                grad[step, s, 0, c] = grad[step, s, 0, c] + in_extra[step, s, c]

            piece(step, GB, s, c).wait_recv()
            total = grad[step, s, 0, c] + in_bottom[step, s, c]
            new = exts[s][0, c, 0:N, :] - STEP_RATE * total
            if step == ITERS - 1:
                out_ref[s, c] = new
            else:
                partly[s, c] = new
                piece(step + 1, FR, s, c).start()

    def finish(step, s):
        for c in range(2):
            piece(step, GR, s, c).wait_recv()
            if step == ITERS - 1:
                out_ref[s, c] = out_ref[s, c] - STEP_RATE * in_side[step, s, c]
            else:
                new = partly[s, c] - STEP_RATE * in_side[step, s, c]
                exts[s][0, c, 0:N, :] = new
                piece(step + 1, FB, s, c).start()

                @pl.when(sends_diagonal)
                def _():
                    piece(step + 1, FX, s, c).start()

                piece(step + 1, FR, s, c).wait_recv()
                exts[s][1, c, 0:N, :] = in_right[s, c] - STEP_RATE * grad[step, s, 1, c]
                pass_side_up(step + 1, s, c)

    for step in range(ITERS):
        if step == 0:
            first_halo(0)
        else:
            take_bottom(step, 0)
        wait_recv(step, FD, 0)
        gather(0)
        if step > 0:
            take_bottom(step, 1)

        p_re, p_im = for_all(probe_ref[0]), for_all(probe_ref[1])
        h_re, h_im = for_all(prop[0]), for_all(prop[1])
        o_re, o_im = win[0, 0], win[0, 1]
        re, im = p_re * o_re - p_im * o_im, p_re * o_im + p_im * o_re
        re, im = lines(re, im, FORWARD)
        re, im = columns(re, im, FORWARD)
        if step == 0:
            first_halo(1)
        re, im = re * h_re - im * h_im, re * h_im + im * h_re
        re, im = columns(re, im, INVERSE)
        re, im = lines(re, im, INVERSE)
        wave[0] = re
        wave[1] = im

        wait_recv(step, FD, 1)
        gather(1)
        w_re, w_im = wave[0], wave[1]
        o_re, o_im = win[1, 0], win[1, 1]
        re, im = w_re * o_re - w_im * o_im, w_re * o_im + w_im * o_re
        re, im = lines(re, im, FORWARD)
        re, im = columns(re, im, FORWARD)
        seen = jnp.concatenate([measured[k] for k in range(SLOTS)], axis=1)
        slot = lax.broadcasted_iota(jnp.int32, (N, SLOTS * N), 1) // N
        factor = 2.0 * (re * re + im * im - seen)
        factor = jnp.where(slot < counts[0, 0], factor, 0.0)
        re, im = columns(re * factor, im * factor, INVERSE)
        re, im = lines(re, im, INVERSE)
        scatter(w_re * re + w_im * im, w_re * im - w_im * re)
        wave[0] = o_re * re + o_im * im
        wave[1] = o_re * im - o_im * re

        send_back(step, 1)
        re, im = lines(wave[0], wave[1], FORWARD)
        re, im = columns(re, im, FORWARD)
        re, im = h_re * re + h_im * im, h_re * im - h_im * re
        re, im = columns(re, im, INVERSE)
        re, im = lines(re, im, INVERSE)
        send_side(step, 1)
        send_turned(step, 1)
        scatter(p_re * re + p_im * im, p_re * im - p_im * re)
        send_back(step, 0)
        if 1 in DETOUR:
            late = row_start & next_col

            @pl.when(late)
            def _():
                send_side(step, 0)
                send_partly(step, 1)

            @pl.when(jnp.logical_not(late))
            def _():
                send_partly(step, 1)
                send_side(step, 0)

        else:
            send_partly(step, 1)
            send_side(step, 0)
        send_turned(step, 0)
        send_partly(step, 0)
        finish(step, 1)
        finish(step, 0)

    wait_send(0, FR, 1)
    wait_send(0, FB, 1)
    for step in range(ITERS):
        for s in range(2):

            @pl.when(jnp.logical_not(row_end & corner_edge(s)))
            def _():
                wait_send(step, GD, s)

            if s in DETOUR:

                @pl.when(row_end & col_start)
                def _():
                    wait_send(step, GE, s)

            @pl.when(corner_diagonal)
            def _():
                wait_send(step, GX, s)

            @pl.when(sends_diagonal)
            def _():
                wait_send(step, FX, s)

            wait_send(step, GB, s)
            wait_send(step, GR, s)
            if step > 0:
                wait_send(step, FR, s)
                wait_send(step, FB, s)

                @pl.when(passes_up(step, s))
                def _():
                    wait_send(step, FD, s)

                if turns(step, s):

                    @pl.when(row_end & next_col)
                    def _():
                        wait_send(step, FE, s)


def per_device(object_slices, probe, phase, positions, counts, measured):
    rights, lefts = dft_tables()
    vmem = pl.BlockSpec(memory_space=pltpu.VMEM)
    hbm = pl.BlockSpec(memory_space=pltpu.HBM)
    f32 = jnp.float32
    return pl.pallas_call(
        functools.partial(kernel, (lax.axis_size("row"), lax.axis_size("col"))),
        out_shape=jax.ShapeDtypeStruct((2, 2, N, N), f32),
        in_specs=[hbm, pl.BlockSpec(memory_space=pl.ANY)] + [hbm] * 6,
        out_specs=vmem,
        scratch_shapes=[
            pltpu.VMEM((2, 2, 2 * N, N), f32),
            pltpu.VMEM((2, 2, 2 * N, N), f32),
            pltpu.VMEM((2, 2, N, SLOTS * N), f32),
            pltpu.VMEM((2, N, SLOTS * N), f32),
            pltpu.VMEM((ITERS, 2, 4, 2, N, N), f32),
            pltpu.VMEM((ITERS, 2, 2, N, N), f32),
            pltpu.VMEM((ITERS, 2, 2, N, N), f32),
            pltpu.VMEM((ITERS, 2, 2, N, N), f32),
            pltpu.VMEM((ITERS, 2, 2, N, N), f32),
            pltpu.VMEM((2, 2, N, N), f32),
            pltpu.VMEM((2, 2, N, N), f32),
            pltpu.VMEM((SLOTS, 2, 3 * N, N), f32),
            pltpu.SMEM((1, 1, 2, SLOTS), jnp.int32),
            pltpu.SMEM((1, 1), jnp.int32),
            pltpu.VMEM((2, N, N), f32),
            pltpu.VMEM((N, N), f32),
            pltpu.VMEM((SLOTS, N, N), f32),
            pltpu.VMEM((2, 6 * N, 2 * N), jnp.bfloat16),
            pltpu.VMEM((2, 2 * N, 6 * N), jnp.bfloat16),
            pltpu.VMEM((2, N, N), f32),
            pltpu.SemaphoreType.DMA((ITERS, 10, 2, 2)),
            pltpu.SemaphoreType.DMA((ITERS, 10, 2, 2)),
            pltpu.SemaphoreType.DMA((9,)),
        ],
        compiler_params=pltpu.CompilerParams(
            collective_id=0, has_side_effects=True, vmem_limit_bytes=56 * 1024 * 1024
        ),
        cost_estimate=pl.CostEstimate(
            flops=6 * 805306368, bytes_accessed=2500000, transcendentals=0
        ),
    )(
        positions.transpose(0, 1, 3, 2),
        counts,
        object_slices,
        probe,
        phase,
        measured.reshape(SLOTS, N, N),
        jnp.asarray(rights),
        jnp.asarray(lefts),
    )


def solution(mesh):
    return jax.shard_map(
        per_device,
        mesh=mesh,
        in_specs=(
            P(None, None, "row", "col"),
            P(),
            P(),
            P("row", "col", None, None),
            P("row", "col"),
            P("row", "col", None, None, None),
        ),
        out_specs=P(None, None, "row", "col"),
        check_vma=False,
    )
```

```python
import functools

import jax
import jax.numpy as jnp
import numpy as np
from jax import lax
from jax.experimental import pallas as pl
from jax.experimental.pallas import tpu as pltpu
from jax.sharding import PartitionSpec as P

ITERS = 2
STEP_RATE = 0.02
MESH = pl.DeviceIdType.MESH
N = 128
SLOTS = 4

FR, FB, FD, GD, GB, GR, FE, GE, FX, GX = range(10)
DETOUR = (0, 1)
RUN = 8
FORWARD, INVERSE = 0, 1


def dft_tables():
    index = np.arange(N)
    angle = (index[:, None] * index[None, :] % N) * (-2.0 * np.pi / N)
    real, imag = np.cos(angle) / np.sqrt(N), np.sin(angle) / np.sqrt(N)
    right = np.block([[real, imag], [-imag, real]]).astype(np.float32)
    rights, lefts = [], []
    for table in (right, right.T):
        high = table.astype(jnp.bfloat16)
        low = (table - high.astype(np.float32)).astype(jnp.bfloat16)
        rights.append(np.concatenate([high, low, high], axis=0))
        lefts.append(np.concatenate([high.T, low.T, high.T], axis=1))
    return np.stack(rights), np.stack(lefts)


def split(value):
    high = value.astype(jnp.bfloat16)
    low = (value - high.astype(jnp.float32)).astype(jnp.bfloat16)
    return high, low


def kernel(
    axes,
    pos_hbm,
    count_hbm,
    obj_hbm,
    probe_hbm,
    phase_hbm,
    measured_hbm,
    rights_hbm,
    lefts_hbm,
    out_ref,
    ext0,
    ext1,
    win,
    wave,
    grad,
    in_corner,
    in_bottom,
    in_side,
    in_extra,
    in_right,
    partly,
    pad,
    positions,
    counts,
    probe_ref,
    phase_ref,
    measured,
    rights,
    lefts,
    prop,
    send_sem,
    recv_sem,
    local_sem,
):
    rows, cols = axes
    row, col = lax.axis_index("row"), lax.axis_index("col")
    left = (row, lax.rem(col + cols - 1, cols))
    right = (row, lax.rem(col + 1, cols))
    above = (lax.rem(row + rows - 1, rows), col)
    below = (lax.rem(row + 1, rows), col)
    above_left, below_right = (above[0], left[1]), (below[0], right[1])
    exts = (ext0, ext1)

    row_end, row_start = lax.rem(row, RUN) == RUN - 1, lax.rem(row, RUN) == 0
    col_end, col_start = lax.rem(col, RUN) == RUN - 1, lax.rem(col, RUN) == 0
    next_col = lax.rem(col, RUN) == 1
    sends_diagonal = row_start & col_start
    corner_diagonal = row_end & col_end

    def turns(step, s):
        return step > 0 and s in DETOUR

    def passes_up(step, s):
        return jnp.logical_not(
            row_start & (col_end | col_start if turns(step, s) else col_end)
        )

    def corner_edge(s):
        return col_end | col_start if s in DETOUR else col_end

    barrier = pltpu.get_barrier_semaphore()
    for neighbour in (left, right, above, below):
        pl.semaphore_signal(barrier, inc=1, device_id=neighbour, device_id_type=MESH)
    for takes_part, neighbour in (
        (sends_diagonal, above_left),
        (corner_diagonal, below_right),
    ):

        @pl.when(takes_part)
        def _():
            pl.semaphore_signal(
                barrier, inc=1, device_id=neighbour, device_id_type=MESH
            )


    def local(source, target, sem):
        return pltpu.make_async_copy(source, target, local_sem.at[sem])

    small_copies = [
        local(pos_hbm, positions, 5),
        local(count_hbm, counts, 6),
        local(probe_hbm, probe_ref, 7),
        local(phase_hbm, phase_ref, 8),
    ]
    own_copies = [local(obj_hbm.at[s], exts[s].at[0, :, 0:N, :], s) for s in range(2)]
    table_copies = [local(rights_hbm, rights, 2), local(lefts_hbm, lefts, 3)]
    measured_copy = local(measured_hbm, measured, 4)
    argument_copies = small_copies + own_copies + table_copies + [measured_copy]
    for copy in argument_copies:
        copy.start()

    def piece(step, kind, s, c):
        ext = exts[s]
        side, bottom = ext.at[1, c, 0:N, :], ext.at[0, c, N : 2 * N, :]
        corner, own = ext.at[1, c, N : 2 * N, :], ext.at[0, c, 0:N, :]
        source, target, device = {
            FR: (partly.at[s, c], in_right.at[s, c], left)
            if step
            else (obj_hbm.at[s, c], side, left),
            FB: (own if step else obj_hbm.at[s, c], bottom, above),
            FD: (side, corner, above),
            FE: (bottom, corner, left),
            GD: (grad.at[step, s, 3, c], in_corner.at[step, s, c], below),
            FX: (own if step else obj_hbm.at[s, c], corner, above_left),
            GX: (grad.at[step, s, 3, c], in_extra.at[step, s, c], below_right),
            GE: (grad.at[step, s, 3, c], in_extra.at[step, s, c], right),
            GB: (grad.at[step, s, 2, c], in_bottom.at[step, s, c], below),
            GR: (grad.at[step, s, 1, c], in_side.at[step, s, c], right),
        }[kind]
        landing = {FE: FD, FX: FD, GX: GE}.get(kind, kind)
        return pltpu.make_async_remote_copy(
            src_ref=source,
            dst_ref=target,
            send_sem=send_sem.at[step, kind, s, c],
            recv_sem=recv_sem.at[step, landing, s, c],
            device_id=device,
            device_id_type=MESH,
        )

    def start(step, kind, s):
        for c in range(2):
            piece(step, kind, s, c).start()

    def wait_send(step, kind, s):
        for c in range(2):
            piece(step, kind, s, c).wait_send()

    def wait_recv(step, kind, s):
        for c in range(2):
            piece(step, kind, s, c).wait_recv()

    lane = lax.broadcasted_iota(jnp.int32, (N, N), 1)

    def gather(s):
        ext = exts[s]
        for k in range(SLOTS):
            p, q = positions[0, 0, 0, k], positions[0, 0, 1, k]
            back = (N - q) & (N - 1)
            for c in range(2):
                near = ext[0, c, pl.ds(p, N), :]
                far = ext[1, c, pl.ds(p, N), :]
                mixed = pltpu.roll(jnp.where(lane >= q, near, far), back, 1)
                win[s, c, :, k * N : (k + 1) * N] = mixed

    def scatter_slot(k, c, value):
        pad[k, c, N : 2 * N, :] = pltpu.roll(value, positions[0, 0, 1, k], 1)

    def collect(step, s, v):
        for c in range(2):
            near = far = None
            for k in range(SLOTS):
                q = positions[0, 0, 1, k]
                moved = pad[k, c, pl.ds((v + 1) * N - positions[0, 0, 0, k], N), :]
                first = jnp.where(lane >= q, moved, 0.0)
                second = jnp.where(lane < q, moved, 0.0)
                near = first if near is None else near + first
                far = second if far is None else far + second
            grad[step, s, 2 * v, c] = near
            grad[step, s, 2 * v + 1, c] = far

    def columns(re, im, which):
        high, low = split(jnp.concatenate([re, im], axis=0))
        stacked = jnp.concatenate([high, high, low], axis=0)
        out = jnp.dot(lefts[which], stacked, preferred_element_type=jnp.float32)
        return out[:N], out[N:]

    def lines(re, im, which):
        block = jnp.concatenate(
            [
                jnp.concatenate([re[:, part], im[:, part]], axis=1)
                for part in (slice(k * N, (k + 1) * N) for k in range(SLOTS))
            ],
            axis=0,
        )
        high, low = split(block)
        stacked = jnp.concatenate([high, high, low], axis=1)
        out = jnp.dot(stacked, rights[which], preferred_element_type=jnp.float32)
        return tuple(
            jnp.concatenate(
                [out[k * N : (k + 1) * N, part] for k in range(SLOTS)], axis=1
            )
            for part in (slice(0, N), slice(N, 2 * N))
        )

    def for_all(value):
        return jnp.concatenate([value] * SLOTS, axis=1)

    def scatter(re, im):
        for k in range(SLOTS):
            scatter_slot(k, 0, re[:, k * N : (k + 1) * N])
            scatter_slot(k, 1, im[:, k * N : (k + 1) * N])

    pl.semaphore_wait(barrier, jnp.where(sends_diagonal | corner_diagonal, 5, 4))

    def send_diagonal(step, s):
        @pl.when(sends_diagonal)
        def _():
            start(step, FX, s)

    start(0, FR, 0)
    start(0, FB, 0)
    send_diagonal(0, 0)
    start(0, FR, 1)
    start(0, FB, 1)
    send_diagonal(0, 1)

    for copy in argument_copies:
        copy.wait()
    prop[0] = jnp.cos(phase_ref[...])
    prop[1] = jnp.sin(phase_ref[...])
    zero = jnp.zeros((N, N), jnp.float32)
    for k in range(SLOTS):
        for c in range(2):
            pad[k, c, 0:N, :] = zero
            pad[k, c, 2 * N : 3 * N, :] = zero

    wait_send(0, FB, 0)
    wait_send(0, FR, 0)

    def pass_side_up(step, s, c):
        @pl.when(passes_up(step, s))
        def _():
            piece(step, FD, s, c).start()

    def take_bottom(step, s):
        for c in range(2):
            piece(step, FB, s, c).wait_recv()
            if turns(step, s):

                @pl.when(row_end & next_col)
                def _():
                    piece(step, FE, s, c).start()

    def first_halo(s):
        for c in range(2):
            piece(0, FR, s, c).wait_recv()
            pass_side_up(0, s, c)
        take_bottom(0, s)

    def send_back(step, s):
        if step == 0:
            @pl.when(passes_up(0, s))
            def _():
                wait_send(0, FD, s)

        collect(step, s, 1)

        @pl.when(jnp.logical_not(row_end & corner_edge(s)))
        def _():
            start(step, GD, s)

        @pl.when(corner_diagonal)
        def _():
            start(step, GX, s)

        if s in DETOUR:

            @pl.when(row_end & col_start)
            def _():
                start(step, GE, s)

        if s in DETOUR:

            @pl.when(jnp.logical_not(row_end & next_col))
            def _():
                start(step, GB, s)

        else:
            start(step, GB, s)
        collect(step, s, 0)

    def send_turned(step, s):
        if s in DETOUR:

            @pl.when(row_end & next_col)
            def _():
                for c in range(2):
                    piece(step, GE, s, c).wait_recv()
                    grad[step, s, 2, c] = grad[step, s, 2, c] + in_extra[step, s, c]
                    piece(step, GB, s, c).start()

    def send_side(step, s):
        for c in range(2):

            @pl.when(jnp.logical_not(row_start & corner_edge(s)))
            def _():
                piece(step, GD, s, c).wait_recv()
                grad[step, s, 1, c] = grad[step, s, 1, c] + in_corner[step, s, c]

            piece(step, GR, s, c).start()

    def send_partly(step, s):
        for c in range(2):
            @pl.when(sends_diagonal)
            def _():
                piece(step, GX, s, c).wait_recv()
                grad[step, s, 0, c] = grad[step, s, 0, c] + in_extra[step, s, c]

            piece(step, GB, s, c).wait_recv()
            total = grad[step, s, 0, c] + in_bottom[step, s, c]
            new = exts[s][0, c, 0:N, :] - STEP_RATE * total
            if step == ITERS - 1:
                out_ref[s, c] = new
            else:
                partly[s, c] = new
                piece(step + 1, FR, s, c).start()

    def finish(step, s):
        for c in range(2):
            piece(step, GR, s, c).wait_recv()
            if step == ITERS - 1:
                out_ref[s, c] = out_ref[s, c] - STEP_RATE * in_side[step, s, c]
            else:
                new = partly[s, c] - STEP_RATE * in_side[step, s, c]
                exts[s][0, c, 0:N, :] = new
                piece(step + 1, FB, s, c).start()

                @pl.when(sends_diagonal)
                def _():
                    piece(step + 1, FX, s, c).start()

                piece(step + 1, FR, s, c).wait_recv()
                exts[s][1, c, 0:N, :] = in_right[s, c] - STEP_RATE * grad[step, s, 1, c]
                pass_side_up(step + 1, s, c)

    for step in range(ITERS):
        if step == 0:
            first_halo(0)
        else:
            take_bottom(step, 0)
        wait_recv(step, FD, 0)
        gather(0)
        if step > 0:
            take_bottom(step, 1)

        p_re, p_im = for_all(probe_ref[0]), for_all(probe_ref[1])
        h_re, h_im = for_all(prop[0]), for_all(prop[1])
        o_re, o_im = win[0, 0], win[0, 1]
        re, im = p_re * o_re - p_im * o_im, p_re * o_im + p_im * o_re
        re, im = lines(re, im, FORWARD)
        re, im = columns(re, im, FORWARD)
        if step == 0:
            first_halo(1)
        re, im = re * h_re - im * h_im, re * h_im + im * h_re
        re, im = columns(re, im, INVERSE)
        re, im = lines(re, im, INVERSE)
        wave[0] = re
        wave[1] = im

        wait_recv(step, FD, 1)
        gather(1)
        w_re, w_im = wave[0], wave[1]
        o_re, o_im = win[1, 0], win[1, 1]
        re, im = w_re * o_re - w_im * o_im, w_re * o_im + w_im * o_re
        re, im = lines(re, im, FORWARD)
        re, im = columns(re, im, FORWARD)
        seen = jnp.concatenate([measured[k] for k in range(SLOTS)], axis=1)
        slot = lax.broadcasted_iota(jnp.int32, (N, SLOTS * N), 1) // N
        factor = 2.0 * (re * re + im * im - seen)
        factor = jnp.where(slot < counts[0, 0], factor, 0.0)
        re, im = columns(re * factor, im * factor, INVERSE)
        re, im = lines(re, im, INVERSE)
        scatter(w_re * re + w_im * im, w_re * im - w_im * re)
        wave[0] = o_re * re + o_im * im
        wave[1] = o_re * im - o_im * re

        send_back(step, 1)
        re, im = lines(wave[0], wave[1], FORWARD)
        re, im = columns(re, im, FORWARD)
        re, im = h_re * re + h_im * im, h_re * im - h_im * re
        re, im = columns(re, im, INVERSE)
        re, im = lines(re, im, INVERSE)
        send_side(step, 1)
        send_turned(step, 1)
        scatter(p_re * re + p_im * im, p_re * im - p_im * re)
        send_back(step, 0)
        if 1 in DETOUR:
            late = row_start & next_col

            @pl.when(late)
            def _():
                send_side(step, 0)
                send_partly(step, 1)

            @pl.when(jnp.logical_not(late))
            def _():
                send_partly(step, 1)
                send_side(step, 0)

        else:
            send_partly(step, 1)
            send_side(step, 0)
        send_turned(step, 0)
        send_partly(step, 0)
        finish(step, 1)
        finish(step, 0)

    wait_send(0, FR, 1)
    wait_send(0, FB, 1)
    for step in range(ITERS):
        for s in range(2):

            @pl.when(jnp.logical_not(row_end & corner_edge(s)))
            def _():
                wait_send(step, GD, s)

            if s in DETOUR:

                @pl.when(row_end & col_start)
                def _():
                    wait_send(step, GE, s)

            @pl.when(corner_diagonal)
            def _():
                wait_send(step, GX, s)

            @pl.when(sends_diagonal)
            def _():
                wait_send(step, FX, s)

            wait_send(step, GB, s)
            wait_send(step, GR, s)
            if step > 0:
                wait_send(step, FR, s)
                wait_send(step, FB, s)

                @pl.when(passes_up(step, s))
                def _():
                    wait_send(step, FD, s)

                if turns(step, s):

                    @pl.when(row_end & next_col)
                    def _():
                        wait_send(step, FE, s)


def per_device(object_slices, probe, phase, positions, counts, measured):
    rights, lefts = dft_tables()
    vmem = pl.BlockSpec(memory_space=pltpu.VMEM)
    hbm = pl.BlockSpec(memory_space=pltpu.HBM)
    f32 = jnp.float32
    return pl.pallas_call(
        functools.partial(kernel, (lax.axis_size("row"), lax.axis_size("col"))),
        out_shape=jax.ShapeDtypeStruct((2, 2, N, N), f32),
        in_specs=[hbm, pl.BlockSpec(memory_space=pl.ANY)] + [hbm] * 6,
        out_specs=vmem,
        scratch_shapes=[
            pltpu.VMEM((2, 2, 2 * N, N), f32),
            pltpu.VMEM((2, 2, 2 * N, N), f32),
            pltpu.VMEM((2, 2, N, SLOTS * N), f32),
            pltpu.VMEM((2, N, SLOTS * N), f32),
            pltpu.VMEM((ITERS, 2, 4, 2, N, N), f32),
            pltpu.VMEM((ITERS, 2, 2, N, N), f32),
            pltpu.VMEM((ITERS, 2, 2, N, N), f32),
            pltpu.VMEM((ITERS, 2, 2, N, N), f32),
            pltpu.VMEM((ITERS, 2, 2, N, N), f32),
            pltpu.VMEM((2, 2, N, N), f32),
            pltpu.VMEM((2, 2, N, N), f32),
            pltpu.VMEM((SLOTS, 2, 3 * N, N), f32),
            pltpu.SMEM((1, 1, 2, SLOTS), jnp.int32),
            pltpu.SMEM((1, 1), jnp.int32),
            pltpu.VMEM((2, N, N), f32),
            pltpu.VMEM((N, N), f32),
            pltpu.VMEM((SLOTS, N, N), f32),
            pltpu.VMEM((2, 6 * N, 2 * N), jnp.bfloat16),
            pltpu.VMEM((2, 2 * N, 6 * N), jnp.bfloat16),
            pltpu.VMEM((2, N, N), f32),
            pltpu.SemaphoreType.DMA((ITERS, 10, 2, 2)),
            pltpu.SemaphoreType.DMA((ITERS, 10, 2, 2)),
            pltpu.SemaphoreType.DMA((9,)),
        ],
        compiler_params=pltpu.CompilerParams(
            collective_id=0, has_side_effects=True, vmem_limit_bytes=56 * 1024 * 1024
        ),
        cost_estimate=pl.CostEstimate(
            flops=6 * 805306368, bytes_accessed=2500000, transcendentals=0
        ),
    )(
        positions.transpose(0, 1, 3, 2),
        counts,
        object_slices,
        probe,
        phase,
        measured.reshape(SLOTS, N, N),
        jnp.asarray(rights),
        jnp.asarray(lefts),
    )


def solution(mesh):
    return jax.shard_map(
        per_device,
        mesh=mesh,
        in_specs=(
            P(None, None, "row", "col"),
            P(),
            P(),
            P("row", "col", None, None),
            P("row", "col"),
            P("row", "col", None, None, None),
        ),
        out_specs=P(None, None, "row", "col"),
        check_vma=False,
    )
```

```python
import functools

import jax
import jax.numpy as jnp
import numpy as np
from jax import lax
from jax.experimental import pallas as pl
from jax.experimental.pallas import tpu as pltpu
from jax.sharding import PartitionSpec as P

ITERS = 2
STEP_RATE = 0.02
MESH = pl.DeviceIdType.MESH
N = 128
SLOTS = 4

FR, FB, FD, GD, GB, GR, FE, GE, FX, GX = range(10)
DETOUR = (0, 1)
RUN = 8
FORWARD, INVERSE = 0, 1


def dft_tables():
    index = np.arange(N)
    angle = (index[:, None] * index[None, :] % N) * (-2.0 * np.pi / N)
    real, imag = np.cos(angle) / np.sqrt(N), np.sin(angle) / np.sqrt(N)
    right = np.block([[real, imag], [-imag, real]]).astype(np.float32)
    rights, lefts = [], []
    for table in (right, right.T):
        high = table.astype(jnp.bfloat16)
        low = (table - high.astype(np.float32)).astype(jnp.bfloat16)
        rights.append(np.concatenate([high, low, high], axis=0))
        lefts.append(np.concatenate([high.T, low.T, high.T], axis=1))
    return np.stack(rights), np.stack(lefts)


def split(value):
    high = value.astype(jnp.bfloat16)
    low = (value - high.astype(jnp.float32)).astype(jnp.bfloat16)
    return high, low


def kernel(
    axes,
    pos_hbm,
    count_hbm,
    obj_hbm,
    probe_hbm,
    phase_hbm,
    measured_hbm,
    rights_hbm,
    lefts_hbm,
    out_ref,
    ext0,
    ext1,
    win,
    wave,
    grad,
    in_corner,
    in_bottom,
    in_side,
    in_extra,
    in_right,
    partly,
    pad,
    positions,
    counts,
    probe_ref,
    phase_ref,
    measured,
    rights,
    lefts,
    prop,
    send_sem,
    recv_sem,
    local_sem,
):
    rows, cols = axes
    row, col = lax.axis_index("row"), lax.axis_index("col")
    left = (row, lax.rem(col + cols - 1, cols))
    right = (row, lax.rem(col + 1, cols))
    above = (lax.rem(row + rows - 1, rows), col)
    below = (lax.rem(row + 1, rows), col)
    above_left, below_right = (above[0], left[1]), (below[0], right[1])
    exts = (ext0, ext1)

    row_end, row_start = lax.rem(row, RUN) == RUN - 1, lax.rem(row, RUN) == 0
    col_end, col_start = lax.rem(col, RUN) == RUN - 1, lax.rem(col, RUN) == 0
    next_col = lax.rem(col, RUN) == 1
    sends_diagonal = row_start & col_start
    corner_diagonal = row_end & col_end

    def turns(step, s):
        return step > 0 and s in DETOUR

    def passes_up(step, s):
        return jnp.logical_not(
            row_start & (col_end | col_start if turns(step, s) else col_end)
        )

    def corner_edge(s):
        return col_end | col_start if s in DETOUR else col_end

    barrier = pltpu.get_barrier_semaphore()
    for neighbour in (left, right, above, below):
        pl.semaphore_signal(barrier, inc=1, device_id=neighbour, device_id_type=MESH)
    for takes_part, neighbour in (
        (sends_diagonal, above_left),
        (corner_diagonal, below_right),
    ):

        @pl.when(takes_part)
        def _():
            pl.semaphore_signal(
                barrier, inc=1, device_id=neighbour, device_id_type=MESH
            )


    def local(source, target, sem):
        return pltpu.make_async_copy(source, target, local_sem.at[sem])

    small_copies = [
        local(pos_hbm, positions, 5),
        local(count_hbm, counts, 6),
        local(probe_hbm, probe_ref, 7),
        local(phase_hbm, phase_ref, 8),
    ]
    own_copies = [local(obj_hbm.at[s], exts[s].at[0, :, 0:N, :], s) for s in range(2)]
    table_copies = [local(rights_hbm, rights, 2), local(lefts_hbm, lefts, 3)]
    measured_copy = local(measured_hbm, measured, 4)
    argument_copies = small_copies + own_copies + table_copies + [measured_copy]
    for copy in argument_copies:
        copy.start()

    def piece(step, kind, s, c):
        ext = exts[s]
        side, bottom = ext.at[1, c, 0:N, :], ext.at[0, c, N : 2 * N, :]
        corner, own = ext.at[1, c, N : 2 * N, :], ext.at[0, c, 0:N, :]
        source, target, device = {
            FR: (partly.at[s, c], in_right.at[s, c], left)
            if step
            else (obj_hbm.at[s, c], side, left),
            FB: (own if step else obj_hbm.at[s, c], bottom, above),
            FD: (side, corner, above),
            FE: (bottom, corner, left),
            GD: (grad.at[step, s, 3, c], in_corner.at[step, s, c], below),
            FX: (own if step else obj_hbm.at[s, c], corner, above_left),
            GX: (grad.at[step, s, 3, c], in_extra.at[step, s, c], below_right),
            GE: (grad.at[step, s, 3, c], in_extra.at[step, s, c], right),
            GB: (grad.at[step, s, 2, c], in_bottom.at[step, s, c], below),
            GR: (grad.at[step, s, 1, c], in_side.at[step, s, c], right),
        }[kind]
        landing = {FE: FD, FX: FD, GX: GE}.get(kind, kind)
        return pltpu.make_async_remote_copy(
            src_ref=source,
            dst_ref=target,
            send_sem=send_sem.at[step, kind, s, c],
            recv_sem=recv_sem.at[step, landing, s, c],
            device_id=device,
            device_id_type=MESH,
        )

    def start(step, kind, s):
        for c in range(2):
            piece(step, kind, s, c).start()

    def wait_send(step, kind, s):
        for c in range(2):
            piece(step, kind, s, c).wait_send()

    def wait_recv(step, kind, s):
        for c in range(2):
            piece(step, kind, s, c).wait_recv()

    lane = lax.broadcasted_iota(jnp.int32, (N, N), 1)

    def gather(s):
        ext = exts[s]
        for k in range(SLOTS):
            p, q = positions[0, 0, 0, k], positions[0, 0, 1, k]
            back = (N - q) & (N - 1)
            for c in range(2):
                near = ext[0, c, pl.ds(p, N), :]
                far = ext[1, c, pl.ds(p, N), :]
                mixed = pltpu.roll(jnp.where(lane >= q, near, far), back, 1)
                win[s, c, :, k * N : (k + 1) * N] = mixed

    def scatter_slot(k, c, value):
        pad[k, c, N : 2 * N, :] = pltpu.roll(value, positions[0, 0, 1, k], 1)

    def collect(step, s, v):
        for c in range(2):
            near = far = None
            for k in range(SLOTS):
                q = positions[0, 0, 1, k]
                moved = pad[k, c, pl.ds((v + 1) * N - positions[0, 0, 0, k], N), :]
                first = jnp.where(lane >= q, moved, 0.0)
                second = jnp.where(lane < q, moved, 0.0)
                near = first if near is None else near + first
                far = second if far is None else far + second
            grad[step, s, 2 * v, c] = near
            grad[step, s, 2 * v + 1, c] = far

    def columns(re, im, which):
        high, low = split(jnp.concatenate([re, im], axis=0))
        stacked = jnp.concatenate([high, high, low], axis=0)
        out = jnp.dot(lefts[which], stacked, preferred_element_type=jnp.float32)
        return out[:N], out[N:]

    def lines(re, im, which):
        block = jnp.concatenate(
            [
                jnp.concatenate([re[:, part], im[:, part]], axis=1)
                for part in (slice(k * N, (k + 1) * N) for k in range(SLOTS))
            ],
            axis=0,
        )
        high, low = split(block)
        stacked = jnp.concatenate([high, high, low], axis=1)
        out = jnp.dot(stacked, rights[which], preferred_element_type=jnp.float32)
        return tuple(
            jnp.concatenate(
                [out[k * N : (k + 1) * N, part] for k in range(SLOTS)], axis=1
            )
            for part in (slice(0, N), slice(N, 2 * N))
        )

    def for_all(value):
        return jnp.concatenate([value] * SLOTS, axis=1)

    def scatter(re, im):
        for k in range(SLOTS):
            scatter_slot(k, 0, re[:, k * N : (k + 1) * N])
            scatter_slot(k, 1, im[:, k * N : (k + 1) * N])

    pl.semaphore_wait(barrier, jnp.where(sends_diagonal | corner_diagonal, 5, 4))

    def send_diagonal(step, s):
        @pl.when(sends_diagonal)
        def _():
            start(step, FX, s)

    start(0, FR, 0)
    start(0, FB, 0)
    send_diagonal(0, 0)
    start(0, FR, 1)
    start(0, FB, 1)
    send_diagonal(0, 1)

    for copy in argument_copies:
        copy.wait()
    prop[0] = jnp.cos(phase_ref[...])
    prop[1] = jnp.sin(phase_ref[...])
    zero = jnp.zeros((N, N), jnp.float32)
    for k in range(SLOTS):
        for c in range(2):
            pad[k, c, 0:N, :] = zero
            pad[k, c, 2 * N : 3 * N, :] = zero

    wait_send(0, FB, 0)
    wait_send(0, FR, 0)

    def pass_side_up(step, s, c):
        @pl.when(passes_up(step, s))
        def _():
            piece(step, FD, s, c).start()

    def take_bottom(step, s):
        for c in range(2):
            piece(step, FB, s, c).wait_recv()
            if turns(step, s):

                @pl.when(row_end & next_col)
                def _():
                    piece(step, FE, s, c).start()

    def first_halo(s):
        for c in range(2):
            piece(0, FR, s, c).wait_recv()
            pass_side_up(0, s, c)
        take_bottom(0, s)

    def send_back(step, s):
        if step == 0:
            @pl.when(passes_up(0, s))
            def _():
                wait_send(0, FD, s)

        collect(step, s, 1)

        @pl.when(jnp.logical_not(row_end & corner_edge(s)))
        def _():
            start(step, GD, s)

        @pl.when(corner_diagonal)
        def _():
            start(step, GX, s)

        if s in DETOUR:

            @pl.when(row_end & col_start)
            def _():
                start(step, GE, s)

        if s in DETOUR:

            @pl.when(jnp.logical_not(row_end & next_col))
            def _():
                start(step, GB, s)

        else:
            start(step, GB, s)
        collect(step, s, 0)

    def send_turned(step, s):
        if s in DETOUR:

            @pl.when(row_end & next_col)
            def _():
                for c in range(2):
                    piece(step, GE, s, c).wait_recv()
                    grad[step, s, 2, c] = grad[step, s, 2, c] + in_extra[step, s, c]
                    piece(step, GB, s, c).start()

    def send_side(step, s):
        for c in range(2):

            @pl.when(jnp.logical_not(row_start & corner_edge(s)))
            def _():
                piece(step, GD, s, c).wait_recv()
                grad[step, s, 1, c] = grad[step, s, 1, c] + in_corner[step, s, c]

            piece(step, GR, s, c).start()

    def send_partly(step, s):
        for c in range(2):
            @pl.when(sends_diagonal)
            def _():
                piece(step, GX, s, c).wait_recv()
                grad[step, s, 0, c] = grad[step, s, 0, c] + in_extra[step, s, c]

            piece(step, GB, s, c).wait_recv()
            total = grad[step, s, 0, c] + in_bottom[step, s, c]
            new = exts[s][0, c, 0:N, :] - STEP_RATE * total
            if step == ITERS - 1:
                out_ref[s, c] = new
            else:
                partly[s, c] = new
                piece(step + 1, FR, s, c).start()

    def finish(step, s):
        for c in range(2):
            piece(step, GR, s, c).wait_recv()
            if step == ITERS - 1:
                out_ref[s, c] = out_ref[s, c] - STEP_RATE * in_side[step, s, c]
            else:
                new = partly[s, c] - STEP_RATE * in_side[step, s, c]
                exts[s][0, c, 0:N, :] = new
                piece(step + 1, FB, s, c).start()

                @pl.when(sends_diagonal)
                def _():
                    piece(step + 1, FX, s, c).start()

                piece(step + 1, FR, s, c).wait_recv()
                exts[s][1, c, 0:N, :] = in_right[s, c] - STEP_RATE * grad[step, s, 1, c]
                pass_side_up(step + 1, s, c)

    for step in range(ITERS):
        if step == 0:
            first_halo(0)
        else:
            take_bottom(step, 0)
        wait_recv(step, FD, 0)
        gather(0)
        if step > 0:
            take_bottom(step, 1)

        p_re, p_im = for_all(probe_ref[0]), for_all(probe_ref[1])
        h_re, h_im = for_all(prop[0]), for_all(prop[1])
        o_re, o_im = win[0, 0], win[0, 1]
        re, im = p_re * o_re - p_im * o_im, p_re * o_im + p_im * o_re
        re, im = lines(re, im, FORWARD)
        re, im = columns(re, im, FORWARD)
        re, im = re * h_re - im * h_im, re * h_im + im * h_re
        re, im = columns(re, im, INVERSE)
        if step == 0:
            first_halo(1)
        re, im = lines(re, im, INVERSE)
        wave[0] = re
        wave[1] = im

        wait_recv(step, FD, 1)
        gather(1)
        w_re, w_im = wave[0], wave[1]
        o_re, o_im = win[1, 0], win[1, 1]
        re, im = w_re * o_re - w_im * o_im, w_re * o_im + w_im * o_re
        re, im = lines(re, im, FORWARD)
        re, im = columns(re, im, FORWARD)
        seen = jnp.concatenate([measured[k] for k in range(SLOTS)], axis=1)
        slot = lax.broadcasted_iota(jnp.int32, (N, SLOTS * N), 1) // N
        factor = 2.0 * (re * re + im * im - seen)
        factor = jnp.where(slot < counts[0, 0], factor, 0.0)
        re, im = columns(re * factor, im * factor, INVERSE)
        re, im = lines(re, im, INVERSE)
        scatter(w_re * re + w_im * im, w_re * im - w_im * re)
        wave[0] = o_re * re + o_im * im
        wave[1] = o_re * im - o_im * re

        send_back(step, 1)
        re, im = lines(wave[0], wave[1], FORWARD)
        re, im = columns(re, im, FORWARD)
        re, im = h_re * re + h_im * im, h_re * im - h_im * re
        re, im = columns(re, im, INVERSE)
        re, im = lines(re, im, INVERSE)
        send_side(step, 1)
        send_turned(step, 1)
        scatter(p_re * re + p_im * im, p_re * im - p_im * re)
        send_back(step, 0)
        if step == ITERS - 1:
            send_side(step, 0)
            send_turned(step, 0)
            send_partly(step, 1)
        elif 1 in DETOUR:
            late = row_start & next_col

            @pl.when(late)
            def _():
                send_side(step, 0)
                send_partly(step, 1)

            @pl.when(jnp.logical_not(late))
            def _():
                send_partly(step, 1)
                send_side(step, 0)

        else:
            send_partly(step, 1)
            send_side(step, 0)
        if step < ITERS - 1:
            send_turned(step, 0)
        send_partly(step, 0)
        finish(step, 1)
        finish(step, 0)

    wait_send(0, FR, 1)
    wait_send(0, FB, 1)
    for step in range(ITERS):
        for s in range(2):

            @pl.when(jnp.logical_not(row_end & corner_edge(s)))
            def _():
                wait_send(step, GD, s)

            if s in DETOUR:

                @pl.when(row_end & col_start)
                def _():
                    wait_send(step, GE, s)

            @pl.when(corner_diagonal)
            def _():
                wait_send(step, GX, s)

            @pl.when(sends_diagonal)
            def _():
                wait_send(step, FX, s)

            wait_send(step, GB, s)
            wait_send(step, GR, s)
            if step > 0:
                wait_send(step, FR, s)
                wait_send(step, FB, s)

                @pl.when(passes_up(step, s))
                def _():
                    wait_send(step, FD, s)

                if turns(step, s):

                    @pl.when(row_end & next_col)
                    def _():
                        wait_send(step, FE, s)


def per_device(object_slices, probe, phase, positions, counts, measured):
    rights, lefts = dft_tables()
    vmem = pl.BlockSpec(memory_space=pltpu.VMEM)
    hbm = pl.BlockSpec(memory_space=pltpu.HBM)
    f32 = jnp.float32
    return pl.pallas_call(
        functools.partial(kernel, (lax.axis_size("row"), lax.axis_size("col"))),
        out_shape=jax.ShapeDtypeStruct((2, 2, N, N), f32),
        in_specs=[hbm, pl.BlockSpec(memory_space=pl.ANY)] + [hbm] * 6,
        out_specs=vmem,
        scratch_shapes=[
            pltpu.VMEM((2, 2, 2 * N, N), f32),
            pltpu.VMEM((2, 2, 2 * N, N), f32),
            pltpu.VMEM((2, 2, N, SLOTS * N), f32),
            pltpu.VMEM((2, N, SLOTS * N), f32),
            pltpu.VMEM((ITERS, 2, 4, 2, N, N), f32),
            pltpu.VMEM((ITERS, 2, 2, N, N), f32),
            pltpu.VMEM((ITERS, 2, 2, N, N), f32),
            pltpu.VMEM((ITERS, 2, 2, N, N), f32),
            pltpu.VMEM((ITERS, 2, 2, N, N), f32),
            pltpu.VMEM((2, 2, N, N), f32),
            pltpu.VMEM((2, 2, N, N), f32),
            pltpu.VMEM((SLOTS, 2, 3 * N, N), f32),
            pltpu.SMEM((1, 1, 2, SLOTS), jnp.int32),
            pltpu.SMEM((1, 1), jnp.int32),
            pltpu.VMEM((2, N, N), f32),
            pltpu.VMEM((N, N), f32),
            pltpu.VMEM((SLOTS, N, N), f32),
            pltpu.VMEM((2, 6 * N, 2 * N), jnp.bfloat16),
            pltpu.VMEM((2, 2 * N, 6 * N), jnp.bfloat16),
            pltpu.VMEM((2, N, N), f32),
            pltpu.SemaphoreType.DMA((ITERS, 10, 2, 2)),
            pltpu.SemaphoreType.DMA((ITERS, 10, 2, 2)),
            pltpu.SemaphoreType.DMA((9,)),
        ],
        compiler_params=pltpu.CompilerParams(
            collective_id=0, has_side_effects=True, vmem_limit_bytes=56 * 1024 * 1024
        ),
        cost_estimate=pl.CostEstimate(
            flops=6 * 805306368, bytes_accessed=2500000, transcendentals=0
        ),
    )(
        positions.transpose(0, 1, 3, 2),
        counts,
        object_slices,
        probe,
        phase,
        measured.reshape(SLOTS, N, N),
        jnp.asarray(rights),
        jnp.asarray(lefts),
    )


def solution(mesh):
    return jax.shard_map(
        per_device,
        mesh=mesh,
        in_specs=(
            P(None, None, "row", "col"),
            P(),
            P(),
            P("row", "col", None, None),
            P("row", "col"),
            P("row", "col", None, None, None),
        ),
        out_specs=P(None, None, "row", "col"),
        check_vma=False,
    )
```
